128 devices in a mesh: row: 16 (over z, y_hi, core), col: 8 (over y_lo, x).
Axes of the slice: x: 4, y: 4 (y_hi: 2, y_lo: 2; y = y_hi * 2 + y_lo), z: 4, core: 2. Of those that a mesh axis runs over, the one named last changes fastest.
Arguments:
- grad_hidden: bfloat16 [1024, 49152], P('row', 'col'), may hold values from -6 to 6
- pre_act: bfloat16 [1024, 49152], P('row', 'col'), may hold values from -6 to 6
- inputs: bfloat16 [1024, 12288], P('col', 'row'), may hold values from -6 to 6
- weight: bfloat16 [12288, 49152], P('row', 'col'), may hold values from -0.0546875 to 0.0546875
Outputs:
- grad_input: bfloat16 [1024, 12288], P('col', 'row')
- grad_weight: bfloat16 [12288, 49152], P('row', 'col')
The draws below stay inside these ranges and needn't reach their ends.
All inputs are finite; a program needn't handle non-finite values.
Results may differ from the reference program's by a relative error of at most 0.017.
Values may be sent and summed in bfloat16 or wider, within the bound.
A program may use at most 128 MiB of HBM per device.

```python
import math
import jax
import jax.numpy as jnp

D = 12288
F = 49152
TOKENS = 1024
N_COL = 8


def block_scale(stream_key, shape, split, low, largest):
    factor_of = 1.0
    for axis_at, shards_of in split:
        steps = jax.random.uniform(jax.random.fold_in(jax.random.fold_in(stream_key, 6), axis_at), (shards_of,), jnp.float32, low / len(split), largest / len(split))
        factor_of = factor_of * jnp.repeat(jnp.exp(steps), shape[axis_at] // shards_of).reshape((-1,) + (1,) * (len(shape) - 1 - axis_at))
    return factor_of


def centred(stream_key, shape, scale, reach, split=(), kind=jnp.bfloat16):
    entries = jax.random.normal(stream_key, shape, jnp.float32) * scale
    if len(split) > 0:
        entries = block_scale(stream_key, shape, split, -0.22, 0.18) * entries
    return jnp.clip(entries, min=-reach, max=reach).astype(kind)


def setup_inputs(seed: int = 0) -> dict:
    arg_keys = jax.random.split(jax.random.key(seed), 5)
    return {
        "grad_hidden": centred(arg_keys[0], (TOKENS, F), 1.0, 6.0, ((0, 16), (1, 8))),
        "pre_act": centred(arg_keys[1], (TOKENS, F), 1.5, 6.0, ((0, 16), (1, 8))),
        "inputs": centred(arg_keys[2], (TOKENS, D), 1.0, 6.0, ((0, 8), (1, 16))),
        "weight": centred(arg_keys[3], (D, F), D ** -0.5, 0.0546875, ((0, 16), (1, 8))),
    }


def gelu_grad(value):
    coeff = math.sqrt(2.0 / math.pi)
    inner = coeff * (value + 0.044715 * value * value * value)
    tanh_value = jnp.tanh(inner)
    return 0.5 * (1.0 + tanh_value) + 0.5 * value * (1.0 - tanh_value * tanh_value) * coeff * (1.0 + 3.0 * 0.044715 * value * value)

def reference(grad_hidden, pre_act, inputs, weight):
    grad_pre = (grad_hidden.astype(jnp.float32) * gelu_grad(pre_act.astype(jnp.float32))).astype(jnp.bfloat16)
    tile_width = F // N_COL
    total = jnp.zeros((TOKENS, D), jnp.float32)
    for index in range(N_COL):
        panel = grad_pre[:, index * tile_width:(index + 1) * tile_width]
        tile = weight[:, index * tile_width:(index + 1) * tile_width]
        part = jax.lax.dot_general(panel, tile, (((1,), (1,)), ((), ())), preferred_element_type=jnp.float32).astype(jnp.bfloat16)
        total = total + part.astype(jnp.float32)
    grad_input = total.astype(jnp.bfloat16)
    blocks = 8
    width = F // blocks
    pieces = []
    for index in range(blocks):
        column = grad_pre[:, index * width:(index + 1) * width]
        pieces.append(jax.lax.dot_general(inputs, column, (((0,), (0,)), ((), ())), preferred_element_type=jnp.float32).astype(jnp.bfloat16))
    grad_weight = jnp.concatenate(pieces, axis=1)
    return (grad_input, grad_weight)
```

```python
import math

import jax
import jax.numpy as jnp
from jax import lax
from jax.experimental import pallas as pl
from jax.experimental.pallas import tpu as pltpu
from jax.sharding import PartitionSpec as P

NZ = 4
NX = 4
NCH = 6
NA = 4
GROUPS = ((0, 1), (2, 3), (4, 5))
NT = (((1,), (1,)), ((), ()))
NN = (((1,), (0,)), ((), ()))
BF16 = jnp.bfloat16
F32 = jnp.float32


def gelu_grad(value):
    coeff = math.sqrt(2.0 / math.pi)
    inner = coeff * (value + 0.044715 * value * value * value)
    tanh_value = jnp.tanh(inner)
    return 0.5 * (1.0 + tanh_value) + 0.5 * value * (1.0 - tanh_value * tanh_value) * coeff * (
        1.0 + 3.0 * 0.044715 * value * value
    )


def main_kernel(
    g_hbm, v_hbm, x_hbm, w_hbm,
    gi_ref, dw_ref,
    gbuf, vbuf, panel, wbuf, xbuf, xt, acc, sbuf, rx, ysend, yrecv,
    load_sem, w_sem, x_own_sem, send_sem, recv_sem, x_send, x_recv, rs_send, rs_recv, y_sem,
):
    r = lax.axis_index("row")
    c = lax.axis_index("col")
    z, yh, k = r // 4, (r // 2) % 2, r % 2
    yl, x = c // NX, c % NX
    tb = g_hbm.shape[0]
    cw = panel.shape[3]
    ob = x_hbm.shape[0]
    plane_rows = panel.shape[2]

    def at_row(dz, dy, dk):
        return lax.rem(z + dz, NZ) * 4 + lax.rem(yh + dy, 2) * 2 + lax.rem(k + dk, 2)

    def at_col(dyl, dx):
        return lax.rem(yl + dyl, 2) * NX + lax.rem(x + dx, NX)

    z_up, z_dn = (at_row(1, 0, 0), c), (at_row(3, 0, 0), c)
    y_other, core_other = (at_row(0, 1, 0), c), (at_row(0, 0, 1), c)

    loads = []
    for i in range(NCH):
        cols = pl.ds(i * cw, cw)
        pair = (
            pltpu.make_async_copy(g_hbm.at[:, cols], gbuf.at[i], load_sem.at[0, i]),
            pltpu.make_async_copy(v_hbm.at[:, cols], vbuf.at[i], load_sem.at[1, i]),
        )
        for cp in pair:
            cp.start()
        loads.append(pair)
    x_own = pltpu.make_async_copy(x_hbm, xbuf.at[c], x_own_sem)
    x_own.start()
    w_loads = []
    for i in range(NCH):
        cols = pl.ds(i * cw, cw)
        cp = pltpu.make_async_copy(w_hbm.at[:, cols], wbuf.at[:, cols], w_sem.at[i])
        cp.start()
        w_loads.append(cp)

    barrier = pltpu.get_barrier_semaphore()
    partners = [z_up, z_dn, y_other, core_other, (r, at_col(1, 0))]
    partners += [(r, at_col(0, dx)) for dx in (1, 2, 3)]
    for partner in partners:
        pl.semaphore_signal(barrier, inc=1, device_id=partner, device_id_type=pl.DeviceIdType.MESH)
    pl.semaphore_wait(barrier, len(partners))

    sends = []

    def remote(src, dst, s_sem, r_sem, target):
        return pltpu.make_async_remote_copy(
            src_ref=src, dst_ref=dst, send_sem=s_sem, recv_sem=r_sem,
            device_id=target, device_id_type=pl.DeviceIdType.MESH,
        )

    def block(dz, dy, dk, i):
        rows = lax.rem(yh + dy, 2) * (2 * tb) + lax.rem(k + dk, 2) * tb
        return panel.at[i, lax.rem(z + dz, NZ), pl.ds(pl.multiple_of(rows, tb), tb), :]

    def push(dz, dy, i, target, rz, ry, rk):
        here = block(dz, dy, 0, i)
        cp = remote(here, here, send_sem.at[len(sends)], recv_sem.at[rk, ry, rz, i], target)
        cp.start()
        sends.append(cp)

    def got(dz, dy, dk, i):
        here = block(dz, dy, dk, i)
        remote(here, here, send_sem.at[0], recv_sem.at[dk, dy, dz, i], core_other).wait_recv()

    def share(dz, dy, i):
        push(dz, dy, i, core_other, dz, dy, 1)

    def relay(dz, dy, i):
        if dz == 3 and i % 2 == 0:
            push(3, dy, i, z_up, 2, dy, 0)
        if dz == 1 and i % 2 == 1:
            push(1, dy, i, z_dn, 2, dy, 0)

    x_sends = []

    def send_x(cb, target, n, rs):
        cp = remote(xbuf.at[cb], xbuf.at[cb], x_send.at[n], rs, target)
        cp.start()
        x_sends.append(cp)

    def x_got(dyl, dx):
        here = xbuf.at[at_col(dyl, dx)]
        remote(here, here, x_send.at[0], x_recv.at[dyl, dx], core_other).wait_recv()

    for n, i in enumerate((4, 0, 5, 1, 2, 3)):
        for cp in loads[i]:
            cp.wait()
        value = gbuf[i].astype(F32) * gelu_grad(vbuf[i].astype(F32))
        panel[i, z, pl.ds(pl.multiple_of(yh * (2 * tb) + k * tb, tb), tb), :] = value.astype(BF16)
        push(0, 0, i, z_up, 3, 0, 0)
        push(0, 0, i, z_dn, 1, 0, 0)
        if i < NA:
            push(0, 0, i, y_other, 0, 1, 0)
        share(0, 0, i)
    for i in (4, 5):
        push(0, 0, i, y_other, 0, 1, 0)

    x_own.wait()
    send_x(c, (r, at_col(1, 0)), 0, x_recv.at[1, 0])
    for dx in (1, 2, 3):
        send_x(c, (r, at_col(0, dx)), dx, x_recv.at[0, NX - dx])

    def mm1(dz, group, first):
        plane = lax.rem(z + dz, NZ)
        term = None
        for i in GROUPS[group]:
            d = lax.dot_general(
                panel[i, plane], wbuf[:, i * cw:(i + 1) * cw], NT, preferred_element_type=F32
            )
            term = d if term is None else term + d
        acc[plane] = term if first else acc[plane] + term

    def mm2(dz, group, first):
        plane = lax.rem(z + dz, NZ)
        for i in GROUPS[group]:
            cols = slice(i * cw, (i + 1) * cw)
            d = lax.dot_general(xt[plane], panel[i, plane], NN, preferred_element_type=F32)
            dw_ref[:, cols] = d if first else dw_ref[:, cols] + d

    def transpose_x(dz):
        plane = lax.rem(z + dz, NZ)
        for h in range(2):
            xt[plane, :, h * ob:(h + 1) * ob] = xbuf[2 * plane + h].T

    def sib(dz, group, dys=(0, 1)):
        for dy in dys:
            for i in GROUPS[group]:
                got(dz, dy, 1, i)

    def rs_copy(dz, h):
        plane = lax.rem(z + dz, NZ)
        owner_yl = plane // 2
        target_x = 2 * lax.rem(plane, 2) + h
        slot = lax.rem(x - target_x + NX, NX)
        cp = remote(
            sbuf.at[2 * plane + h], rx.at[owner_yl, slot], rs_send.at[dz, h],
            rs_recv.at[owner_yl, slot], (r, yl * NX + target_x),
        )
        return cp, x != target_x

    def rs_start(dz):
        plane = lax.rem(z + dz, NZ)
        for h in range(2):
            sbuf[2 * plane + h] = acc[plane, h * ob:(h + 1) * ob, :].astype(BF16)
            cp, use = rs_copy(dz, h)
            pl.when(use)(cp.start)

    def rs_collect(owner_yl):
        plane = 2 * owner_yl + x // 2
        total = acc[plane, pl.ds(pl.multiple_of(lax.rem(x, 2) * ob, ob), ob), :]
        for slot in (1, 2, 3):
            here = rx.at[owner_yl, slot]
            remote(here, here, rs_send.at[0, 0], rs_recv.at[owner_yl, slot], core_other).wait_recv()
            total = total + rx[owner_yl, slot].astype(F32)
        return total

    for i in range(2):
        for dz in (3, 1):
            got(dz, 0, 0, 4 + i)
            push(dz, 0, 4 + i, y_other, dz, 1, 0)
            relay(dz, 0, 4 + i)
            share(dz, 0, 4 + i)
        got(0, 1, 0, i)
        push(0, 1, i, z_up, 3, 1, 0)
        push(0, 1, i, z_dn, 1, 1, 0)
        share(0, 1, i)
    x_got(1, 0)
    for dx in (1, 2, 3):
        send_x(at_col(1, 0), (r, at_col(0, dx)), 3 + dx, x_recv.at[1, NX - dx])
    for cp in w_loads:
        cp.wait()
    sib(0, 0)
    mm1(0, 0, True)
    for i in (2, 3):
        for dz in (3, 1):
            got(dz, 0, 0, i - 2)
            relay(dz, 0, i - 2)
            share(dz, 0, i - 2)
        got(0, 1, 0, i)
        push(0, 1, i, z_up, 3, 1, 0)
        push(0, 1, i, z_dn, 1, 1, 0)
        share(0, 1, i)
    sib(0, 1)
    mm1(0, 1, False)
    for i in (2, 3):
        for dz in (3, 1):
            got(dz, 0, 0, i)
            relay(dz, 0, i)
            share(dz, 0, i)
        got(0, 1, 0, 2 + i)
        share(0, 1, 2 + i)
    for dyl in range(2):
        for dx in (1, 2, 3):
            x_got(dyl, dx)
    for dz in range(NZ):
        transpose_x(dz)
    sib(0, 2)
    mm1(0, 2, False)
    rs_start(0)
    mm2(0, 0, True)
    got(2, 0, 0, 4)
    push(2, 0, 4, y_other, 2, 1, 0)
    share(2, 0, 4)
    for dz in (3, 1):
        got(dz, 1, 0, 0)
        relay(dz, 1, 0)
        share(dz, 1, 0)
    mm2(0, 1, True)
    got(2, 0, 0, 5)
    push(2, 0, 5, y_other, 2, 1, 0)
    share(2, 0, 5)
    mm2(0, 2, True)
    for dz in (3, 1):
        got(dz, 1, 0, 4)
        share(dz, 1, 4)
        got(dz, 1, 0, 1)
        relay(dz, 1, 1)
        share(dz, 1, 1)
    for dz in (3, 1):
        sib(dz, 0)
        mm1(dz, 0, True)
        mm2(dz, 0, False)
    for dz in (3, 1):
        got(dz, 1, 0, 2)
        relay(dz, 1, 2)
        share(dz, 1, 2)
        got(dz, 1, 0, 5)
        share(dz, 1, 5)
    for dz in (3, 1):
        sib(dz, 2)
        mm1(dz, 2, False)
        if dz == 3:
            for e in (3, 1):
                got(e, 1, 0, 3)
                relay(e, 1, 3)
                share(e, 1, 3)
        mm2(dz, 2, False)
    for i in range(NA):
        got(2, 0, 0, i)
        share(2, 0, i)
    for dz in (3, 1):
        sib(dz, 1)
        mm1(dz, 1, False)
        rs_start(dz)
    for i in (4, 5):
        got(2, 1, 0, i)
        share(2, 1, i)
    mm2(3, 1, False)
    sib(2, 2)
    mm1(2, 2, True)
    for i in (0, 1):
        got(2, 1, 0, i)
        share(2, 1, i)
    mm2(1, 1, False)
    sib(2, 0)
    mm1(2, 0, False)
    for i in (2, 3):
        got(2, 1, 0, i)
        share(2, 1, i)
    sib(2, 1)
    mm1(2, 1, False)
    rs_start(2)
    mm2(2, 0, False)
    mm2(2, 1, False)
    far = 1 - yl
    ysend[...] = rs_collect(far).astype(BF16)
    y_cp = remote(ysend, yrecv, y_sem.at[0], y_sem.at[1], (r, at_col(1, 0)))
    y_cp.start()
    mm2(2, 2, False)
    total = rs_collect(yl)
    y_cp.wait()
    gi_ref[...] = (total + yrecv[...].astype(F32)).astype(gi_ref.dtype)

    for cp in sends:
        cp.wait_send()
    for cp in x_sends:
        cp.wait_send()
    for dz in range(NZ):
        for h in range(2):
            cp, use = rs_copy(dz, h)
            pl.when(use)(cp.wait_send)


N_SENDS = 24 + 6 + 12 + 48
OUT_PARTS = 8


def out_kernel(gi_ref, dw_ref, gi_out, dw_out, buf, sem):
    part = dw_ref.shape[1] // OUT_PARTS
    gi_copy = pltpu.make_async_copy(gi_ref, gi_out, sem.at[OUT_PARTS])
    gi_copy.start()
    copies = []
    for i in range(OUT_PARTS):
        cols = pl.ds(i * part, part)
        buf[:, i * part:(i + 1) * part] = dw_ref[:, i * part:(i + 1) * part].astype(buf.dtype)
        cp = pltpu.make_async_copy(buf.at[:, cols], dw_out.at[:, cols], sem.at[i])
        cp.start()
        copies.append(cp)
    for cp in copies:
        cp.wait()
    gi_copy.wait()


def body(grad_hidden, pre_act, inputs, weight):
    tb, ft = grad_hidden.shape
    ob, dt = inputs.shape
    cw = ft // NCH
    tokens = 16 * tb
    hbm = pl.BlockSpec(memory_space=pltpu.HBM)
    vmem = pl.BlockSpec(memory_space=pltpu.VMEM)
    dma = pltpu.SemaphoreType.DMA
    gi, dw = pl.pallas_call(
        main_kernel,
        out_shape=(pltpu.VMEM((ob, dt), BF16), pltpu.VMEM((dt, ft), F32)),
        in_specs=[hbm] * 4,
        out_specs=(vmem, vmem),
        scratch_shapes=[
            pltpu.VMEM((NCH, tb, cw), BF16),
            pltpu.VMEM((NCH, tb, cw), BF16),
            pltpu.VMEM((NCH, NZ, tokens // NZ, cw), BF16),
            pltpu.VMEM((dt, ft), BF16),
            pltpu.VMEM((8, ob, dt), BF16),
            pltpu.VMEM((NZ, dt, tokens // NZ), BF16),
            pltpu.VMEM((NZ, tokens // NZ, dt), F32),
            pltpu.VMEM((8, ob, dt), BF16),
            pltpu.VMEM((2, NX, ob, dt), BF16),
            pltpu.VMEM((ob, dt), BF16),
            pltpu.VMEM((ob, dt), BF16),
            dma((2, NCH)),
            dma((NCH,)),
            dma,
            dma((N_SENDS,)),
            dma((2, 2, NZ, NCH)),
            dma((7,)),
            dma((2, NX)),
            dma((NZ, 2)),
            dma((2, NX)),
            dma((2,)),
        ],
        compiler_params=pltpu.CompilerParams(
            collective_id=0, has_side_effects=True, vmem_limit_bytes=44 * 2**20
        ),
        name="gather_and_multiply",
    )(grad_hidden, pre_act, inputs, weight)
    return pl.pallas_call(
        out_kernel,
        out_shape=(
            jax.ShapeDtypeStruct((ob, dt), BF16),
            jax.ShapeDtypeStruct((dt, ft), BF16),
        ),
        in_specs=[vmem, vmem],
        out_specs=(hbm, hbm),
        scratch_shapes=[pltpu.VMEM((dt, ft), BF16), dma((OUT_PARTS + 1,))],
        compiler_params=pltpu.CompilerParams(vmem_limit_bytes=20 * 2**20),
        name="round_and_write",
    )(gi, dw)


def solution(mesh):
    return jax.shard_map(
        body,
        mesh=mesh,
        in_specs=(P("row", "col"), P("row", "col"), P("col", "row"), P("row", "col")),
        out_specs=(P("col", "row"), P("row", "col")),
        check_vma=False,
    )
```

```python
import math

import jax
import jax.numpy as jnp
from jax import lax
from jax.experimental import pallas as pl
from jax.experimental.pallas import tpu as pltpu
from jax.sharding import PartitionSpec as P

NZ = 4
NX = 4
NCH = 6
NA = 4
GROUPS = ((0, 1), (2, 3), (4, 5))
MM1 = (
    (0, 0), (0, 1), (3, 0), (1, 0), (3, 1), (1, 1), (3, 2), (1, 2), (0, 2), None, None, (2, 2), (2, 0), (2, 1),
    None, None,
)
MM2 = (
    None, (0, 0), (0, 1), (3, 0), (1, 0), None, None, (3, 1), (1, 1), (3, 2), (1, 2), (0, 2), None, (2, 2),
    (2, 0), (2, 1),
)
STEPS = len(MM1)
NT = (((1,), (1,)), ((), ()))
NN = (((1,), (0,)), ((), ()))
BF16 = jnp.bfloat16
F32 = jnp.float32


def gelu_grad(value):
    coeff = math.sqrt(2.0 / math.pi)
    inner = coeff * (value + 0.044715 * value * value * value)
    tanh_value = jnp.tanh(inner)
    return 0.5 * (1.0 + tanh_value) + 0.5 * value * (1.0 - tanh_value * tanh_value) * coeff * (
        1.0 + 3.0 * 0.044715 * value * value
    )


def main_kernel(
    g_hbm, v_hbm, x_hbm, w_hbm,
    gi_ref, dw_ref,
    gbuf, vbuf, panel, wbuf, xbuf, xt, acc, sbuf, rx, stage, parts,
    load_sem, w_sem, x_own_sem, send_sem, recv_sem, x_send, x_recv, rs_send, rs_recv, own_send, own_recv,
):
    r = lax.axis_index("row")
    c = lax.axis_index("col")
    z, yh, k = r // 4, (r // 2) % 2, r % 2
    yl, x = c // NX, c % NX
    tb = g_hbm.shape[0]
    cw = panel.shape[3]
    ob = x_hbm.shape[0]
    plane_rows = panel.shape[2]

    def at_row(dz, dy, dk):
        return lax.rem(z + dz, NZ) * 4 + lax.rem(yh + dy, 2) * 2 + lax.rem(k + dk, 2)

    def at_col(dyl, dx):
        return lax.rem(yl + dyl, 2) * NX + lax.rem(x + dx, NX)

    z_up, z_dn = (at_row(1, 0, 0), c), (at_row(3, 0, 0), c)
    y_other, core_other = (at_row(0, 1, 0), c), (at_row(0, 0, 1), c)

    x_own = pltpu.make_async_copy(x_hbm, xbuf.at[c], x_own_sem)
    x_own.start()
    loads = []
    for i in range(NCH):
        cols = pl.ds(i * cw, cw)
        pair = (
            pltpu.make_async_copy(g_hbm.at[:, cols], gbuf.at[i], load_sem.at[0, i]),
            pltpu.make_async_copy(v_hbm.at[:, cols], vbuf.at[i], load_sem.at[1, i]),
        )
        for cp in pair:
            cp.start()
        loads.append(pair)
    barrier = pltpu.get_barrier_semaphore()
    partners = [z_up, z_dn, y_other, core_other, (r, at_col(1, 0))]
    partners += [(r, at_col(0, dx)) for dx in (1, 2, 3)]
    for partner in partners:
        pl.semaphore_signal(barrier, inc=1, device_id=partner, device_id_type=pl.DeviceIdType.MESH)
    pl.semaphore_wait(barrier, len(partners))

    sends = []

    def remote(src, dst, s_sem, r_sem, target):
        return pltpu.make_async_remote_copy(
            src_ref=src, dst_ref=dst, send_sem=s_sem, recv_sem=r_sem,
            device_id=target, device_id_type=pl.DeviceIdType.MESH,
        )

    def block(dz, dy, dk, i):
        rows = lax.rem(yh + dy, 2) * (2 * tb) + lax.rem(k + dk, 2) * tb
        return panel.at[i, lax.rem(z + dz, NZ), pl.ds(pl.multiple_of(rows, tb), tb), :]

    def push(dz, dy, i, target, rz, ry, rk):
        here = block(dz, dy, 0, i)
        remote(here, here, send_sem.at[len(sends)], recv_sem.at[rk, ry, rz, i], target).start()
        sends.append(i)

    def got(dz, dy, dk, i):
        here = block(dz, dy, dk, i)
        remote(here, here, send_sem.at[0], recv_sem.at[dk, dy, dz, i], core_other).wait_recv()

    def share(dz, dy, i):
        push(dz, dy, i, core_other, dz, dy, 1)

    def relay(dz, dy, i):
        if dz == 3 and i % 2 == 0:
            push(3, dy, i, z_up, 2, dy, 0)
        if dz == 1 and i % 2 == 1:
            push(1, dy, i, z_dn, 2, dy, 0)

    def send_x(cb, target, n, rs):
        remote(xbuf.at[cb], xbuf.at[cb], x_send.at[n], rs, target).start()

    def x_got(dyl, dx):
        here = xbuf.at[at_col(dyl, dx)]
        remote(here, here, x_send.at[0], x_recv.at[dyl, dx], core_other).wait_recv()

    x_own.wait()
    send_x(c, (r, at_col(1, 0)), 0, x_recv.at[1, 0])
    for dx in (1, 2, 3):
        send_x(c, (r, at_col(0, dx)), dx, x_recv.at[0, NX - dx])

    for i in range(NCH):
        for cp in loads[i]:
            cp.wait()
        value = gbuf[i].astype(F32) * gelu_grad(vbuf[i].astype(F32))
        panel[i, z, pl.ds(pl.multiple_of(yh * (2 * tb) + k * tb, tb), tb), :] = value.astype(BF16)
        push(0, 0, i, z_up, 3, 0, 0)
        push(0, 0, i, z_dn, 1, 0, 0)
        if i < NA:
            push(0, 0, i, y_other, 0, 1, 0)
        share(0, 0, i)

    w_loads = []
    for i in range(NCH):
        cols = pl.ds(i * cw, cw)
        cp = pltpu.make_async_copy(w_hbm.at[:, cols], wbuf.at[i], w_sem.at[i])
        cp.start()
        w_loads.append(cp)

    def packed(values, step):
        word = sum(v << (2 * n) for n, v in enumerate(values))
        return lax.shift_right_arithmetic(jnp.int32(word - (1 << 32) if word >> 31 else word), 2 * step) & 3

    def unit(units, step):
        dz = packed([u[0] if u else 0 for u in units], step)
        return lax.rem(z + dz, NZ), packed([u[1] if u else 0 for u in units], step)

    def busy(units, step):
        return packed([0 if u is None else 1 for u in units], step) == 1

    def choose(step, what, lo, hi):
        if hi - lo == 1:
            what(lo)
        else:
            mid = (lo + hi) // 2
            lax.cond(
                step < mid, lambda: choose(step, what, lo, mid), lambda: choose(step, what, mid, hi)
            )

    def mm1(step):
        plane, group = unit(MM1, step)
        term = None
        for j in range(2):
            i = 2 * group + j
            d = lax.dot_general(panel[i, plane], wbuf[i], NT, preferred_element_type=F32)
            term = d if term is None else term + d
        acc[plane] = acc[plane] + term

    def mm2(step):
        plane, group = unit(MM2, step)
        for j in range(2):
            i = 2 * group + j
            d = lax.dot_general(xt[plane], panel[i, plane], NN, preferred_element_type=F32)
            dw_ref[i] = dw_ref[i] + d

    def transpose_x(dz):
        plane = lax.rem(z + dz, NZ)
        for h in range(2):
            xt[plane, :, h * ob:(h + 1) * ob] = xbuf[2 * plane + h].T

    def sib(dz, group, dys=(0, 1)):
        for dy in dys:
            for i in GROUPS[group]:
                got(dz, dy, 1, i)

    def quarter(plane, xc):
        near = xc // 2 == lax.rem(plane, 2)
        half = jnp.where(near, lax.rem(xc, 2), 1 - lax.rem(xc, 2))
        return pl.multiple_of(half * ob + jnp.where(near, 0, tb), tb)

    def rs_copy(dz, dx):
        plane = lax.rem(z + dz, NZ)
        rows = pl.ds(quarter(plane, lax.rem(x + dx, NX)), tb)
        return remote(
            sbuf.at[plane, rows, :], rx.at[dz, dx - 1], rs_send.at[dz, dx - 1], rs_recv.at[dz, dx - 1],
            (r, at_col(0, dx)),
        )

    def rs_start(dz):
        plane = lax.rem(z + dz, NZ)
        sbuf[plane] = acc[plane].astype(BF16)
        for dx in (1, 2, 3):
            rs_copy(dz, dx).start()

    def own_copy(dz):
        plane = lax.rem(z + dz, NZ)
        near = x // 2 == lax.rem(plane, 2)
        j = jnp.where(near, 0, 1)
        owner_x = jnp.where(near, x, 3 - x)
        owner_yl = plane // 2
        rel = lax.rem(owner_yl + yl, 2)
        cp = remote(
            stage.at[dz], parts.at[j, rel], own_send.at[dz], own_recv.at[j, rel], (r, owner_yl * NX + owner_x)
        )
        return cp, jnp.logical_or(owner_x != x, owner_yl != yl)

    def rs_collect(dz):
        plane = lax.rem(z + dz, NZ)
        total = acc[plane, pl.ds(quarter(plane, x), tb), :]
        for dx in (1, 2, 3):
            rs_copy(dz, dx).wait_recv()
            total = total + rx[dz, dx - 1].astype(F32)
        stage[dz] = total.astype(BF16)
        cp, away = own_copy(dz)
        pl.when(away)(cp.start)

    def rs_finish():
        mine = lax.rem(c // 2 - z + NZ, NZ)
        for j in range(2):
            for rel in range(2):
                if j or rel:
                    here = parts.at[j, rel]
                    remote(here, here, own_send.at[0], own_recv.at[j, rel], core_other).wait_recv()
            first = parts[1, 0] if j else stage[mine]
            total = first.astype(F32) + parts[j, 1].astype(F32)
            gi_ref[j * tb:(j + 1) * tb, :] = total.astype(gi_ref.dtype)

    def near(i):
        for dz in (3, 1):
            got(dz, 0, 0, i)
            if i >= NA:
                push(dz, 0, i, y_other, dz, 1, 0)
            share(dz, 0, i)

    def other(i):
        got(0, 1, 0, i)
        if i < NA:
            push(0, 1, i, z_up, 3, 1, 0)
            push(0, 1, i, z_dn, 1, 1, 0)
        share(0, 1, i)

    def near_other(i):
        for dz in (3, 1):
            got(dz, 1, 0, i)
            if i < NA:
                relay(dz, 1, i)
            share(dz, 1, i)

    def far(i):
        got(2, 0, 0, i)
        if i >= NA:
            push(2, 0, i, y_other, 2, 1, 0)
        share(2, 0, i)

    def far_other(i):
        got(2, 1, 0, i)
        share(2, 1, i)

    def forward_x():
        x_got(1, 0)
        for dx in (1, 2, 3):
            send_x(at_col(1, 0), (r, at_col(0, dx)), 3 + dx, x_recv.at[1, NX - dx])

    def clear(chunks):
        for i in chunks:
            dw_ref[i] = jnp.zeros_like(dw_ref[i])

    def before(n):
        if n == 0:
            acc[...] = jnp.zeros_like(acc)
            near(0)
            other(0)
            forward_x()
            clear((0, 1))
            near(1)
            other(1)
            clear((2, 3))
            for cp in w_loads:
                cp.wait()
        if n == 1:
            near(2)
            clear((4, 5))
            near(3)
            other(2)
            near(4)
            other(3)
            near(5)
            for i in (4, 5):
                push(0, 0, i, y_other, 0, 1, 0)
            for i in (4, 5, 0, 1, 2, 3):
                for dz in (3, 1):
                    relay(dz, 0, i)
        if n == 2:
            near_other(0)
            near_other(1)
        if n == 4:
            near_other(2)
            near_other(3)
        if n == 5:
            near_other(4)
            near_other(5)
        if n == 6:
            far(4)
            far(5)
        if n == 7:
            other(4)
            other(5)
        if n == 9:
            far(0)
            far(1)
        if n == 10:
            far(2)
            far(3)
        if n == 11:
            far_other(4)
            far_other(5)
            far_other(0)
            far_other(1)
        if n == 12:
            far_other(2)
            far_other(3)
        if MM1[n] is not None:
            sib(*MM1[n])
        if n == 14:
            rs_collect(0)

    def between(n):
        if n == 1:
            for dyl in range(2):
                for dx in (1, 2, 3):
                    x_got(dyl, dx)
            for dz in range(NZ):
                transpose_x(dz)
        for dz, last in ((3, 6), (1, 7), (0, 8), (2, 13)):
            if n == last:
                rs_start(dz)
        if n == 13:
            rs_collect(3)
            rs_collect(1)

    @pl.loop(0, STEPS)
    def _(step):
        choose(step, before, 0, STEPS)
        pl.when(busy(MM1, step))(lambda: mm1(step))
        choose(step, between, 0, STEPS)
        pl.when(busy(MM2, step))(lambda: mm2(step))

    rs_collect(2)
    rs_finish()

    for n in range(len(sends)):
        here = block(0, 0, 0, 0)
        remote(here, here, send_sem.at[n], recv_sem.at[0, 0, 0, 0], core_other).wait_send()
    for n in range(7):
        remote(xbuf.at[c], xbuf.at[c], x_send.at[n], x_recv.at[0, 0], core_other).wait_send()
    for dz in range(NZ):
        for dx in (1, 2, 3):
            rs_copy(dz, dx).wait_send()
        cp, away = own_copy(dz)
        pl.when(away)(cp.wait_send)


N_SENDS = 24 + 6 + 12 + 48


def out_kernel(gi_ref, dw_ref, gi_out, dw_out, buf, sem):
    cw = dw_ref.shape[2]
    gi_copy = pltpu.make_async_copy(gi_ref, gi_out, sem.at[NCH])
    gi_copy.start()
    copies = []
    for i in range(NCH):
        buf[i] = dw_ref[i].astype(buf.dtype)
        cp = pltpu.make_async_copy(buf.at[i], dw_out.at[:, pl.ds(i * cw, cw)], sem.at[i])
        cp.start()
        copies.append(cp)
    for cp in copies:
        cp.wait()
    gi_copy.wait()


def body(grad_hidden, pre_act, inputs, weight):
    tb, ft = grad_hidden.shape
    ob, dt = inputs.shape
    cw = ft // NCH
    tokens = 16 * tb
    hbm = pl.BlockSpec(memory_space=pltpu.HBM)
    vmem = pl.BlockSpec(memory_space=pltpu.VMEM)
    dma = pltpu.SemaphoreType.DMA
    gi, dw = pl.pallas_call(
        main_kernel,
        out_shape=(pltpu.VMEM((ob, dt), BF16), pltpu.VMEM((NCH, dt, cw), F32)),
        in_specs=[hbm] * 4,
        out_specs=(vmem, vmem),
        scratch_shapes=[
            pltpu.VMEM((NCH, tb, cw), BF16),
            pltpu.VMEM((NCH, tb, cw), BF16),
            pltpu.VMEM((NCH, NZ, tokens // NZ, cw), BF16),
            pltpu.VMEM((NCH, dt, cw), BF16),
            pltpu.VMEM((8, ob, dt), BF16),
            pltpu.VMEM((NZ, dt, tokens // NZ), BF16),
            pltpu.VMEM((NZ, tokens // NZ, dt), F32),
            pltpu.VMEM((NZ, tokens // NZ, dt), BF16),
            pltpu.VMEM((NZ, NX - 1, tb, dt), BF16),
            pltpu.VMEM((NZ, tb, dt), BF16),
            pltpu.VMEM((2, 2, tb, dt), BF16),
            dma((2, NCH)),
            dma((NCH,)),
            dma,
            dma((N_SENDS,)),
            dma((2, 2, NZ, NCH)),
            dma((7,)),
            dma((2, NX)),
            dma((NZ, NX - 1)),
            dma((NZ, NX - 1)),
            dma((NZ,)),
            dma((2, 2)),
        ],
        compiler_params=pltpu.CompilerParams(
            collective_id=0, has_side_effects=True, vmem_limit_bytes=44 * 2**20
        ),
        name="gather_and_multiply",
    )(grad_hidden, pre_act, inputs, weight)
    return pl.pallas_call(
        out_kernel,
        out_shape=(
            jax.ShapeDtypeStruct((ob, dt), BF16),
            jax.ShapeDtypeStruct((dt, ft), BF16),
        ),
        in_specs=[vmem, vmem],
        out_specs=(hbm, hbm),
        scratch_shapes=[pltpu.VMEM((NCH, dt, cw), BF16), dma((NCH + 1,))],
        compiler_params=pltpu.CompilerParams(vmem_limit_bytes=20 * 2**20),
        name="round_and_write",
    )(gi, dw)


def solution(mesh):
    return jax.shard_map(
        body,
        mesh=mesh,
        in_specs=(P("row", "col"), P("row", "col"), P("col", "row"), P("row", "col")),
        out_specs=(P("col", "row"), P("row", "col")),
        check_vma=False,
    )
```

```python
import math

import jax
import jax.numpy as jnp
from jax import lax
from jax.experimental import pallas as pl
from jax.experimental.pallas import tpu as pltpu
from jax.sharding import PartitionSpec as P

NZ = 4
NX = 4
NCH = 6
NA = 4
GROUPS = ((0, 1), (2, 3), (4, 5))
OWN, NEAR, CROSS, FAR = range(4)
STEP = (
    ((NEAR, 0), None, None),
    ((OWN, 0), None, None),
    ((NEAR, 1), None, None),
    ((OWN, 1), None, None),
    ((NEAR, 2), None, (OWN, 0)),
    (None, None, (NEAR, 0)),
    (None, None, (OWN, 1)),
    ((CROSS, 0), None, (NEAR, 1)),
    (None, None, (NEAR, 2)),
    ((OWN, 2), None, (OWN, 2)),
    ((CROSS, 1), None, None),
    ((CROSS, 2), None, (CROSS, 0)),
    (None, (0, 0), None),
    (None, (0, 1), None),
    (None, (0, 2), (CROSS, 1)),
    (None, (1, 2), None),
    (None, (1, 0), None),
    (None, (1, 1), (CROSS, 2)),
    (None, None, (FAR, 2)),
    (None, None, (FAR, 0)),
    (None, None, (FAR, 1)),
)
MM1, MM1H, MM2 = zip(*STEP)
STEPS = len(STEP)
NT = (((1,), (1,)), ((), ()))
NN = (((1,), (0,)), ((), ()))
BF16 = jnp.bfloat16
F32 = jnp.float32


def gelu_grad(value):
    coeff = math.sqrt(2.0 / math.pi)
    inner = coeff * (value + 0.044715 * value * value * value)
    tanh_value = jnp.tanh(inner)
    return 0.5 * (1.0 + tanh_value) + 0.5 * value * (1.0 - tanh_value * tanh_value) * coeff * (
        1.0 + 3.0 * 0.044715 * value * value
    )


def main_kernel(
    g_hbm, v_hbm, x_hbm, w_hbm,
    gi_ref, dw_ref,
    gbuf, vbuf, panel, wbuf, xbuf, xt, acc, acc2, sbuf, rx, stage, parts,
    load_sem, w_sem, x_own_sem, send_sem, recv_sem, far_sem, x_send, x_recv, rs_send, rs_recv, rs2_send, rs2_recv,
    own_send, own2_send, own_recv,
):
    r = lax.axis_index("row")
    c = lax.axis_index("col")
    z, yh, k = r // 4, (r // 2) % 2, r % 2
    yl, x = c // NX, c % NX
    tb = g_hbm.shape[0]
    cw = panel.shape[3]
    ob = x_hbm.shape[0]

    def at_row(dz, dy, dk):
        return lax.rem(z + dz, NZ) * 4 + lax.rem(yh + dy, 2) * 2 + lax.rem(k + dk, 2)

    def at_col(dyl, dx):
        return lax.rem(yl + dyl, 2) * NX + lax.rem(x + dx, NX)

    z_up, z_dn = (at_row(1, 0, 0), c), (at_row(3, 0, 0), c)
    y_other, core_other = (at_row(0, 1, 0), c), (at_row(0, 0, 1), c)

    x_own = pltpu.make_async_copy(x_hbm, xbuf.at[c], x_own_sem)
    x_own.start()
    loads = []
    for i in range(NCH):
        cols = pl.ds(i * cw, cw)
        pair = (
            pltpu.make_async_copy(g_hbm.at[:, cols], gbuf.at[i], load_sem.at[0, i]),
            pltpu.make_async_copy(v_hbm.at[:, cols], vbuf.at[i], load_sem.at[1, i]),
        )
        for cp in pair:
            cp.start()
        loads.append(pair)
    barrier = pltpu.get_barrier_semaphore()
    partners = [z_up, z_dn, y_other, core_other, (r, at_col(1, 0))]
    partners += [(r, at_col(0, dx)) for dx in (1, 2, 3)]
    for partner in partners:
        pl.semaphore_signal(barrier, inc=1, device_id=partner, device_id_type=pl.DeviceIdType.MESH)
    pl.semaphore_wait(barrier, len(partners))

    hb = tb // 2
    n_sent = [0]
    n_sent2 = [0]

    def remote(src, dst, s_sem, r_sem, target):
        return pltpu.make_async_remote_copy(
            src_ref=src, dst_ref=dst, send_sem=s_sem, recv_sem=r_sem,
            device_id=target, device_id_type=pl.DeviceIdType.MESH,
        )

    def owned(dz, dy):
        return 2 * lax.rem(z + dz, NZ) + lax.rem(yh + dy, 2)

    def block(dz, dy, dk, i):
        rows = pl.ds(pl.multiple_of(lax.rem(k + dk, 2) * tb, tb), tb)
        return panel.at[i, owned(dz, dy), rows, :]

    def half(dz, dy, dk, i, p):
        rows = pl.ds(pl.multiple_of(lax.rem(k + dk, 2) * tb + p * hb, hb), hb)
        return panel.at[i, owned(dz, dy), rows, :]

    def push(dz, dy, i, target, rz, ry, rk):
        here = block(dz, dy, 0, i)
        remote(here, here, send_sem.at[n_sent[0]], recv_sem.at[rk, ry, rz, i], target).start()
        n_sent[0] += 1

    def push2(dz, dy, i, p, target, ry, rk):
        here = half(dz, dy, 0, i, p)
        remote(here, here, send_sem.at[N_SENDS + n_sent2[0]], far_sem.at[rk, ry, i, p], target).start()
        n_sent2[0] += 1

    def got(dz, dy, dk, i):
        here = block(dz, dy, dk, i)
        remote(here, here, send_sem.at[0], recv_sem.at[dk, dy, dz, i], core_other).wait_recv()

    def got2(dy, dk, i, p):
        here = half(2, dy, dk, i, p)
        remote(here, here, send_sem.at[0], far_sem.at[dk, dy, i, p], core_other).wait_recv()

    def share(dz, dy, i):
        push(dz, dy, i, core_other, dz, dy, 1)

    def relay(dy, i, p):
        if i % 2 == 0:
            push2(3, dy, i, p, z_up, dy, 0)
        else:
            push2(1, dy, i, p, z_dn, dy, 0)

    def send_x(cb, target, n, rs):
        remote(xbuf.at[cb], xbuf.at[cb], x_send.at[n], rs, target).start()

    def x_got(dyl, dx):
        here = xbuf.at[at_col(dyl, dx)]
        remote(here, here, x_send.at[0], x_recv.at[dyl, dx], core_other).wait_recv()

    x_own.wait()
    send_x(c, (r, at_col(1, 0)), 0, x_recv.at[1, 0])
    for dx in (1, 2, 3):
        send_x(c, (r, at_col(0, dx)), dx, x_recv.at[0, NX - dx])

    for i in range(NCH):
        for cp in loads[i]:
            cp.wait()
        value = gbuf[i].astype(F32) * gelu_grad(vbuf[i].astype(F32))
        panel[i, 2 * z + yh, pl.ds(pl.multiple_of(k * tb, tb), tb), :] = value.astype(BF16)
        push(0, 0, i, z_up, 3, 0, 0)
        push(0, 0, i, z_dn, 1, 0, 0)
        push(0, 0, i, y_other, 0, 1, 0)
        share(0, 0, i)

    w_loads = []
    for i in range(NCH):
        cols = pl.ds(i * cw, cw)
        cp = pltpu.make_async_copy(w_hbm.at[:, cols], wbuf.at[i], w_sem.at[i])
        cp.start()
        w_loads.append(cp)

    def packed(values, step):
        def word(part):
            w = sum(v << (2 * n) for n, v in enumerate(part))
            return jnp.int32(w - (1 << 32) if w >> 31 else w)

        w = jnp.where(step < 16, word(values[:16]), word(values[16:]))
        return lax.shift_right_arithmetic(w, 2 * lax.rem(step, 16)) & 3

    def unit(units, step):
        return packed([u[0] if u else 0 for u in units], step), packed([u[1] if u else 0 for u in units], step)

    def pair(kind):
        def of(own, near, cross, far):
            return jnp.where(kind < 2, jnp.where(kind == 0, own, near), jnp.where(kind == 2, cross, far))

        first = of(2 * z, owned(3, 0), owned(3, 1), 2 * lax.rem(z + 2, NZ))
        second = of(2 * z + 1, owned(1, 0), owned(1, 1), 2 * lax.rem(z + 2, NZ) + 1)
        return first, second

    def busy(units, step):
        return packed([0 if u is None else 1 for u in units], step) == 1

    def choose(step, what, lo, hi):
        if hi - lo == 1:
            what(lo)
        else:
            mid = (lo + hi) // 2
            lax.cond(
                step < mid, lambda: choose(step, what, lo, mid), lambda: choose(step, what, mid, hi)
            )

    def mm1(step):
        kind, group = unit(MM1, step)
        blocks = pair(kind)
        term = None
        for j in range(2):
            i = 2 * group + j
            left = jnp.concatenate([panel[i, cb] for cb in blocks], axis=0)
            d = lax.dot_general(left, wbuf[i], NT, preferred_element_type=F32)
            term = d if term is None else term + d
        for n, cb in enumerate(blocks):
            acc[cb] = acc[cb] + term[n * ob:(n + 1) * ob]

    def mm1h(step):
        p, group = unit(MM1H, step)
        plane = lax.rem(z + 2, NZ)
        term = None
        for j in range(2):
            i = 2 * group + j
            rows = [
                panel[i, 2 * plane + q // 2, pl.ds(pl.multiple_of(q % 2 * tb + p * hb, hb), hb), :] for q in range(4)
            ]
            d = lax.dot_general(jnp.concatenate(rows, axis=0), wbuf[i], NT, preferred_element_type=F32)
            term = d if term is None else term + d
        acc2[p] = acc2[p] + term

    def mm2(step):
        kind, group = unit(MM2, step)
        blocks = pair(kind)
        left = jnp.concatenate([xt[cb] for cb in blocks], axis=1)
        for j in range(2):
            i = 2 * group + j
            right = jnp.concatenate([panel[i, cb] for cb in blocks], axis=0)
            d = lax.dot_general(left, right, NN, preferred_element_type=F32)
            dw_ref[i] = dw_ref[i] + d

    def sib(kind, group):
        offsets = {OWN: ((0, 0), (0, 1)), NEAR: ((3, 0), (1, 0)), CROSS: ((3, 1), (1, 1))}[kind]
        for dz, dy in offsets:
            for i in GROUPS[group]:
                got(dz, dy, 1, i)

    def sib2(p, group):
        for dy in range(2):
            for i in GROUPS[group]:
                got2(dy, 1, i, p)

    def quarter(plane, xc):
        near = xc // 2 == lax.rem(plane, 2)
        side = jnp.where(near, lax.rem(xc, 2), 1 - lax.rem(xc, 2))
        return 2 * plane + side, pl.multiple_of(jnp.where(near, 0, tb), tb)

    def rs_copy(dz, dx):
        plane = lax.rem(z + dz, NZ)
        cb, row = quarter(plane, lax.rem(x + dx, NX))
        return remote(
            sbuf.at[cb, pl.ds(row, tb), :], rx.at[dz, dx - 1], rs_send.at[dz, dx - 1], rs_recv.at[dz, dx - 1],
            (r, at_col(0, dx)),
        )

    def rs_start(dz):
        plane = lax.rem(z + dz, NZ)
        for h in range(2):
            sbuf[2 * plane + h] = acc[2 * plane + h].astype(BF16)
        for dx in (1, 2, 3):
            rs_copy(dz, dx).start()

    def own_copy(dz, p=None):
        plane = lax.rem(z + dz, NZ)
        near = x // 2 == lax.rem(plane, 2)
        j = jnp.where(near, 0, 1)
        owner_x = jnp.where(near, x, 3 - x)
        owner_yl = plane // 2
        rel = lax.rem(owner_yl + yl, 2)
        src, dst, sem = stage.at[dz], parts.at[j, rel], own_send.at[dz]
        if p is not None:
            part = pl.ds(p * hb, hb)
            src, dst, sem = stage.at[dz, part, :], parts.at[j, rel, part, :], own2_send.at[p]
        cp = remote(src, dst, sem, own_recv.at[j, rel], (r, owner_yl * NX + owner_x))
        return cp, jnp.logical_or(owner_x != x, owner_yl != yl)

    def rs_collect(dz):
        plane = lax.rem(z + dz, NZ)
        cb, row = quarter(plane, x)
        total = acc[cb, pl.ds(row, tb), :]
        for dx in (1, 2, 3):
            rs_copy(dz, dx).wait_recv()
            total = total + rx[dz, dx - 1].astype(F32)
        stage[dz] = total.astype(BF16)
        cp, away = own_copy(dz)
        pl.when(away)(cp.start)

    def rs2_copy(p, dx):
        plane = lax.rem(z + 2, NZ)
        cb, row = quarter(plane, lax.rem(x + dx, NX))
        return remote(
            sbuf.at[cb, pl.ds(pl.multiple_of(row + p * hb, hb), hb), :], rx.at[2, dx - 1, pl.ds(p * hb, hb), :],
            rs2_send.at[p, dx - 1], rs2_recv.at[p, dx - 1], (r, at_col(0, dx)),
        )

    def rs2_start(p):
        plane = lax.rem(z + 2, NZ)
        for q in range(4):
            row = q % 2 * tb + p * hb
            sbuf[2 * plane + q // 2, row:row + hb, :] = acc2[p, q * hb:(q + 1) * hb, :].astype(BF16)
        for dx in (1, 2, 3):
            rs2_copy(p, dx).start()

    def rs2_collect(p):
        plane = lax.rem(z + 2, NZ)
        cb, row = quarter(plane, x)
        row = lax.rem(cb, 2) * tb + row // 2
        total = acc2[p, pl.ds(pl.multiple_of(row, hb), hb), :]
        for dx in (1, 2, 3):
            rs2_copy(p, dx).wait_recv()
            total = total + rx[2, dx - 1, p * hb:(p + 1) * hb, :].astype(F32)
        stage[2, p * hb:(p + 1) * hb, :] = total.astype(BF16)
        cp, away = own_copy(2, p)
        pl.when(away)(cp.start)

    def rs_finish():
        mine = lax.rem(c // 2 - z + NZ, NZ)
        for j in range(2):
            for rel in range(2):
                if j or rel:
                    here = parts.at[j, rel]
                    remote(here, here, own_send.at[0], own_recv.at[j, rel], core_other).wait_recv()
            first = parts[1, 0] if j else stage[mine]
            total = first.astype(F32) + parts[j, 1].astype(F32)
            gi_ref[j * tb:(j + 1) * tb, :] = total.astype(gi_ref.dtype)

    def near(i):
        for dz in (3, 1):
            got(dz, 0, 0, i)
            if i >= NA:
                push(dz, 0, i, y_other, dz, 1, 0)
            share(dz, 0, i)

    def other(i):
        got(0, 1, 0, i)
        if i < NA:
            push(0, 1, i, z_up, 3, 1, 0)
            push(0, 1, i, z_dn, 1, 1, 0)
        share(0, 1, i)

    def near_other(i):
        for dz in (3, 1):
            got(dz, 1, 0, i)
            share(dz, 1, i)
        if i < NA:
            relay(1, i, 0)

    def far(i, p):
        got2(0, 0, i, p)
        if i >= NA:
            push2(2, 0, i, p, y_other, 1, 0)
        push2(2, 0, i, p, core_other, 0, 1)

    def far_other(i, p):
        got2(1, 0, i, p)
        push2(2, 1, i, p, core_other, 1, 1)

    def forward_x():
        x_got(1, 0)
        for dx in (1, 2, 3):
            send_x(at_col(1, 0), (r, at_col(0, dx)), 3 + dx, x_recv.at[1, NX - dx])

    def clear(chunks):
        for i in chunks:
            dw_ref[i] = jnp.zeros_like(dw_ref[i])

    def before(n):
        if n == 0:
            acc[...] = jnp.zeros_like(acc)
            acc2[...] = jnp.zeros_like(acc2)
            near(0)
            forward_x()
            clear((0, 1))
            near(1)
            for cp in w_loads:
                cp.wait()
        if n == 1:
            other(0)
            near(2)
            other(1)
            clear((2, 3))
        if n == 2:
            near(3)
            other(2)
        if n == 3:
            near(4)
            other(3)
            clear((4, 5))
        if n == 4:
            near(5)
            for i in (4, 5):
                for p in range(2):
                    relay(0, i, p)
            for i in range(NA):
                relay(0, i, 0)
        if n == 6:
            near_other(0)
        if n == 7:
            near_other(1)
        if n == 8:
            other(4)
            other(5)
            near_other(2)
        if n == 9:
            near_other(3)
            for dy in range(2):
                for i in range(NA):
                    relay(dy, i, 1)
        if n == 10:
            near_other(4)
        if n == 11:
            near_other(5)
            for p in range(2):
                far(4, p)
                far(5, p)
            for i in range(NA):
                far(i, 0)
        if n == 12:
            far_other(2, 0)
            far_other(3, 0)
        if n == 13:
            far_other(4, 0)
            far_other(5, 0)
        if n == 14:
            for i in range(NA):
                far(i, 1)
        if n == 15:
            far_other(0, 1)
            far_other(1, 1)
        if n == 16:
            far_other(2, 1)
            far_other(3, 1)
        if MM1[n] is not None:
            sib(*MM1[n])
        if MM1H[n] is not None:
            sib2(*MM1H[n])
        if n == 13:
            rs_collect(0)
        if n == 19:
            rs2_collect(0)
        if n == 20:
            rs2_collect(1)

    def between(n):
        if n == 4:
            for dyl in range(2):
                for dx in (1, 2, 3):
                    x_got(dyl, dx)
            for cb in range(2 * NZ):
                xt[cb] = xbuf[cb].T
        if n == 9:
            rs_start(0)
        if n == 11:
            rs_start(3)
            rs_start(1)
            far_other(0, 0)
            far_other(1, 0)
        if n == 14:
            rs2_start(0)
            far_other(4, 1)
            far_other(5, 1)
        if n == 16:
            rs_collect(3)
        if n == 17:
            rs2_start(1)
            rs_collect(1)

    @pl.loop(0, STEPS)
    def _(step):
        choose(step, before, 0, STEPS)
        pl.when(busy(MM1, step))(lambda: mm1(step))
        pl.when(busy(MM1H, step))(lambda: mm1h(step))
        choose(step, between, 0, STEPS)
        pl.when(busy(MM2, step))(lambda: mm2(step))

    rs_finish()

    assert n_sent[0] == N_SENDS and n_sent2[0] == N_SENDS2
    for n in range(N_SENDS):
        here = block(0, 0, 0, 0)
        remote(here, here, send_sem.at[n], recv_sem.at[0, 0, 0, 0], core_other).wait_send()
    for n in range(N_SENDS2):
        here = half(0, 0, 0, 0, 0)
        remote(here, here, send_sem.at[N_SENDS + n], recv_sem.at[0, 0, 0, 0], core_other).wait_send()
    for n in range(7):
        remote(xbuf.at[c], xbuf.at[c], x_send.at[n], x_recv.at[0, 0], core_other).wait_send()
    for dz in (0, 3, 1):
        for dx in (1, 2, 3):
            rs_copy(dz, dx).wait_send()
        cp, away = own_copy(dz)
        pl.when(away)(cp.wait_send)
    for p in range(2):
        for dx in (1, 2, 3):
            rs2_copy(p, dx).wait_send()
        cp, away = own_copy(2, p)
        pl.when(away)(cp.wait_send)


N_SENDS = (12 + 8) + (6 + 4) + 36
N_SENDS2 = 20 + 4 + 24


def out_kernel(gi_ref, dw_ref, gi_out, dw_out, buf, sem):
    cw = dw_ref.shape[2]
    gi_copy = pltpu.make_async_copy(gi_ref, gi_out, sem.at[NCH])
    gi_copy.start()
    copies = []
    for i in range(NCH):
        buf[i] = dw_ref[i].astype(buf.dtype)
        cp = pltpu.make_async_copy(buf.at[i], dw_out.at[:, pl.ds(i * cw, cw)], sem.at[i])
        cp.start()
        copies.append(cp)
    for cp in copies:
        cp.wait()
    gi_copy.wait()


def body(grad_hidden, pre_act, inputs, weight):
    tb, ft = grad_hidden.shape
    ob, dt = inputs.shape
    cw = ft // NCH
    hbm = pl.BlockSpec(memory_space=pltpu.HBM)
    vmem = pl.BlockSpec(memory_space=pltpu.VMEM)
    dma = pltpu.SemaphoreType.DMA
    gi, dw = pl.pallas_call(
        main_kernel,
        out_shape=(pltpu.VMEM((ob, dt), BF16), pltpu.VMEM((NCH, dt, cw), F32)),
        in_specs=[hbm] * 4,
        out_specs=(vmem, vmem),
        scratch_shapes=[
            pltpu.VMEM((NCH, tb, cw), BF16),
            pltpu.VMEM((NCH, tb, cw), BF16),
            pltpu.VMEM((NCH, 8, ob, cw), BF16),
            pltpu.VMEM((NCH, dt, cw), BF16),
            pltpu.VMEM((8, ob, dt), BF16),
            pltpu.VMEM((8, dt, ob), BF16),
            pltpu.VMEM((8, ob, dt), F32),
            pltpu.VMEM((2, ob, dt), F32),
            pltpu.VMEM((8, ob, dt), BF16),
            pltpu.VMEM((NZ, NX - 1, tb, dt), BF16),
            pltpu.VMEM((NZ, tb, dt), BF16),
            pltpu.VMEM((2, 2, tb, dt), BF16),
            dma((2, NCH)),
            dma((NCH,)),
            dma,
            dma((N_SENDS + N_SENDS2,)),
            dma((2, 2, NZ, NCH)),
            dma((2, 2, NCH, 2)),
            dma((7,)),
            dma((2, NX)),
            dma((NZ, NX - 1)),
            dma((NZ, NX - 1)),
            dma((2, NX - 1)),
            dma((2, NX - 1)),
            dma((NZ,)),
            dma((2,)),
            dma((2, 2)),
        ],
        compiler_params=pltpu.CompilerParams(
            collective_id=0, has_side_effects=True, vmem_limit_bytes=44 * 2**20
        ),
        name="gather_and_multiply",
    )(grad_hidden, pre_act, inputs, weight)
    return pl.pallas_call(
        out_kernel,
        out_shape=(
            jax.ShapeDtypeStruct((ob, dt), BF16),
            jax.ShapeDtypeStruct((dt, ft), BF16),
        ),
        in_specs=[vmem, vmem],
        out_specs=(hbm, hbm),
        scratch_shapes=[pltpu.VMEM((NCH, dt, cw), BF16), dma((NCH + 1,))],
        compiler_params=pltpu.CompilerParams(vmem_limit_bytes=20 * 2**20),
        name="round_and_write",
    )(gi, dw)


def solution(mesh):
    return jax.shard_map(
        body,
        mesh=mesh,
        in_specs=(P("row", "col"), P("row", "col"), P("col", "row"), P("row", "col")),
        out_specs=(P("col", "row"), P("row", "col")),
        check_vma=False,
    )
```

```python
import math

import jax
import jax.numpy as jnp
from jax import lax
from jax.experimental import pallas as pl
from jax.experimental.pallas import tpu as pltpu
from jax.sharding import PartitionSpec as P

NZ = 4
NX = 4
NCH = 6
NA = 4
GROUPS = ((0, 1), (2, 3), (4, 5))
OWN, NEAR, CROSS, FAR = range(4)
STEP = (
    ((NEAR, 0), None, None),
    ((OWN, 0), None, None),
    ((NEAR, 1), None, None),
    ((OWN, 1), None, (OWN, 0)),
    ((NEAR, 2), None, (NEAR, 0)),
    (None, None, (OWN, 1)),
    (None, None, (NEAR, 1)),
    ((CROSS, 0), None, (NEAR, 2)),
    ((OWN, 2), None, (OWN, 2)),
    (None, None, (CROSS, 0)),
    ((CROSS, 1), None, (CROSS, 1)),
    ((CROSS, 2), None, (CROSS, 2)),
    (None, (0, 0), None),
    (None, (0, 1), None),
    (None, (0, 2), None),
    (None, (1, 2), None),
    (None, (1, 0), None),
    (None, (1, 1), None),
    (None, None, (FAR, 2)),
    (None, None, (FAR, 0)),
    (None, None, (FAR, 1)),
)
MM1, MM1H, MM2 = zip(*STEP)
STEPS = len(STEP)
NT = (((1,), (1,)), ((), ()))
NN = (((1,), (0,)), ((), ()))
BF16 = jnp.bfloat16
F32 = jnp.float32


def gelu_grad(value):
    coeff = math.sqrt(2.0 / math.pi)
    inner = coeff * (value + 0.044715 * value * value * value)
    tanh_value = jnp.tanh(inner)
    return 0.5 * (1.0 + tanh_value) + 0.5 * value * (1.0 - tanh_value * tanh_value) * coeff * (
        1.0 + 3.0 * 0.044715 * value * value
    )


def main_kernel(
    g_hbm, v_hbm, x_hbm, w_hbm,
    gi_ref, dw_ref,
    gbuf, vbuf, panel, wbuf, xbuf, xt, acc, acc2, sbuf, rx, stage, parts,
    load_sem, w_sem, x_own_sem, send_sem, recv_sem, far_sem, x_send, x_recv, rs_send, rs_recv, rs2_send, rs2_recv,
    own_send, own_recv,
):
    r = lax.axis_index("row")
    c = lax.axis_index("col")
    z, yh, k = r // 4, (r // 2) % 2, r % 2
    yl, x = c // NX, c % NX
    tb = g_hbm.shape[0]
    cw = panel.shape[3]
    ob = x_hbm.shape[0]

    def at_row(dz, dy, dk):
        return lax.rem(z + dz, NZ) * 4 + lax.rem(yh + dy, 2) * 2 + lax.rem(k + dk, 2)

    def at_col(dyl, dx):
        return lax.rem(yl + dyl, 2) * NX + lax.rem(x + dx, NX)

    z_up, z_dn = (at_row(1, 0, 0), c), (at_row(3, 0, 0), c)
    y_other, core_other = (at_row(0, 1, 0), c), (at_row(0, 0, 1), c)

    x_own = pltpu.make_async_copy(x_hbm, xbuf.at[c], x_own_sem)
    x_own.start()
    loads = []
    for i in range(NCH):
        cols = pl.ds(i * cw, cw)
        pair = (
            pltpu.make_async_copy(g_hbm.at[:, cols], gbuf.at[i], load_sem.at[0, i]),
            pltpu.make_async_copy(v_hbm.at[:, cols], vbuf.at[i], load_sem.at[1, i]),
        )
        for cp in pair:
            cp.start()
        loads.append(pair)
    barrier = pltpu.get_barrier_semaphore()
    partners = [z_up, z_dn, y_other, core_other, (r, at_col(1, 0))]
    partners += [(r, at_col(0, dx)) for dx in (1, 2, 3)]
    for partner in partners:
        pl.semaphore_signal(barrier, inc=1, device_id=partner, device_id_type=pl.DeviceIdType.MESH)

    def grad_pre(i):
        for cp in loads[i]:
            cp.wait()
        value = gbuf[i].astype(F32) * gelu_grad(vbuf[i].astype(F32))
        panel[i, 2 * z + yh, pl.ds(pl.multiple_of(k * tb, tb), tb), :] = value.astype(BF16)

    grad_pre(0)
    pl.semaphore_wait(barrier, len(partners))

    hb = tb // 2
    n_sent = [0]
    n_sent2 = [0]

    def remote(src, dst, s_sem, r_sem, target):
        return pltpu.make_async_remote_copy(
            src_ref=src, dst_ref=dst, send_sem=s_sem, recv_sem=r_sem,
            device_id=target, device_id_type=pl.DeviceIdType.MESH,
        )

    def owned(dz, dy):
        return 2 * lax.rem(z + dz, NZ) + lax.rem(yh + dy, 2)

    def block(dz, dy, dk, i):
        rows = pl.ds(pl.multiple_of(lax.rem(k + dk, 2) * tb, tb), tb)
        return panel.at[i, owned(dz, dy), rows, :]

    def half(dz, dy, dk, i, p):
        rows = pl.ds(pl.multiple_of(lax.rem(k + dk, 2) * tb + p * hb, hb), hb)
        return panel.at[i, owned(dz, dy), rows, :]

    def push(dz, dy, i, target, rz, ry, rk):
        here = block(dz, dy, 0, i)
        remote(here, here, send_sem.at[n_sent[0]], recv_sem.at[rk, ry, rz, i], target).start()
        n_sent[0] += 1

    def push2(dz, dy, i, p, target, ry, rk):
        here = half(dz, dy, 0, i, p)
        remote(here, here, send_sem.at[N_SENDS + n_sent2[0]], far_sem.at[rk, ry, i, p], target).start()
        n_sent2[0] += 1

    def got(dz, dy, dk, i):
        here = block(dz, dy, dk, i)
        remote(here, here, send_sem.at[0], recv_sem.at[dk, dy, dz, i], core_other).wait_recv()

    def got2(dy, dk, i, p):
        here = half(2, dy, dk, i, p)
        remote(here, here, send_sem.at[0], far_sem.at[dk, dy, i, p], core_other).wait_recv()

    def share(dz, dy, i):
        push(dz, dy, i, core_other, dz, dy, 1)

    def relay(dy, i, p):
        if i % 2 == 0:
            push2(3, dy, i, p, z_up, dy, 0)
        else:
            push2(1, dy, i, p, z_dn, dy, 0)

    def send_x(cb, target, n, rs):
        remote(xbuf.at[cb], xbuf.at[cb], x_send.at[n], rs, target).start()

    def x_got(dyl, dx):
        here = xbuf.at[at_col(dyl, dx)]
        remote(here, here, x_send.at[0], x_recv.at[dyl, dx], core_other).wait_recv()

    x_own.wait()
    send_x(c, (r, at_col(1, 0)), 0, x_recv.at[1, 0])
    for dx in (1, 2, 3):
        send_x(c, (r, at_col(0, dx)), dx, x_recv.at[0, NX - dx])

    for i in range(NCH):
        if i:
            grad_pre(i)
        push(0, 0, i, z_up, 3, 0, 0)
        push(0, 0, i, z_dn, 1, 0, 0)
        push(0, 0, i, y_other, 0, 1, 0)
        share(0, 0, i)

    w_loads = []
    for i in range(NCH):
        cols = pl.ds(i * cw, cw)
        cp = pltpu.make_async_copy(w_hbm.at[:, cols], wbuf.at[i], w_sem.at[i])
        cp.start()
        w_loads.append(cp)

    def packed(values, step):
        def word(part):
            w = sum(v << (2 * n) for n, v in enumerate(part))
            return jnp.int32(w - (1 << 32) if w >> 31 else w)

        w = jnp.where(step < 16, word(values[:16]), word(values[16:]))
        return lax.shift_right_arithmetic(w, 2 * lax.rem(step, 16)) & 3

    def unit(units, step):
        return packed([u[0] if u else 0 for u in units], step), packed([u[1] if u else 0 for u in units], step)

    def pair(kind):
        def of(own, near, cross, far):
            return jnp.where(kind < 2, jnp.where(kind == 0, own, near), jnp.where(kind == 2, cross, far))

        first = of(2 * z, owned(3, 0), owned(3, 1), 2 * lax.rem(z + 2, NZ))
        second = of(2 * z + 1, owned(1, 0), owned(1, 1), 2 * lax.rem(z + 2, NZ) + 1)
        return first, second

    def busy(units, step):
        return packed([0 if u is None else 1 for u in units], step) == 1

    def choose(step, what, lo, hi):
        if hi - lo == 1:
            what(lo)
        else:
            mid = (lo + hi) // 2
            lax.cond(
                step < mid, lambda: choose(step, what, lo, mid), lambda: choose(step, what, mid, hi)
            )

    def mm1(step):
        kind, group = unit(MM1, step)
        blocks = pair(kind)
        term = None
        for j in range(2):
            i = 2 * group + j
            left = jnp.concatenate([panel[i, cb] for cb in blocks], axis=0)
            d = lax.dot_general(left, wbuf[i], NT, preferred_element_type=F32)
            term = d if term is None else term + d
        for n, cb in enumerate(blocks):
            acc[cb] = acc[cb] + term[n * ob:(n + 1) * ob]

    def mm1h(step):
        p, group = unit(MM1H, step)
        plane = lax.rem(z + 2, NZ)
        term = None
        for j in range(2):
            i = 2 * group + j
            rows = [
                panel[i, 2 * plane + q // 2, pl.ds(pl.multiple_of(q % 2 * tb + p * hb, hb), hb), :] for q in range(4)
            ]
            d = lax.dot_general(jnp.concatenate(rows, axis=0), wbuf[i], NT, preferred_element_type=F32)
            term = d if term is None else term + d
        acc2[p] = acc2[p] + term

    def mm2(step):
        kind, group = unit(MM2, step)
        blocks = pair(kind)
        left = jnp.concatenate([xt[cb] for cb in blocks], axis=1)
        for j in range(2):
            i = 2 * group + j
            right = jnp.concatenate([panel[i, cb] for cb in blocks], axis=0)
            d = lax.dot_general(left, right, NN, preferred_element_type=F32)
            dw_ref[i] = dw_ref[i] + d

    def sib(kind, group):
        offsets = {OWN: ((0, 0), (0, 1)), NEAR: ((3, 0), (1, 0)), CROSS: ((3, 1), (1, 1))}[kind]
        for dz, dy in offsets:
            for i in GROUPS[group]:
                got(dz, dy, 1, i)

    def sib2(p, group):
        for dy in range(2):
            for i in GROUPS[group]:
                got2(dy, 1, i, p)

    def quarter(kind, xc):
        near = xc // 2 == lax.rem(z + (kind in (NEAR, CROSS)), 2)
        h = jnp.where(near, lax.rem(xc, 2), 1 - lax.rem(xc, 2))
        row = pl.multiple_of(jnp.where(near, 0, tb), tb)
        if kind in (OWN, FAR):
            return 2 * lax.rem(z + kind // FAR * 2, NZ) + h, row
        dy = kind - NEAR
        return jnp.where(h == lax.rem(yh + dy, 2), owned(3, dy), owned(1, dy)), row

    def rs_copy(kind, dx):
        cb, row = quarter(kind, lax.rem(x + dx, NX))
        return remote(
            sbuf.at[cb, pl.ds(row, tb), :], rx.at[kind, dx - 1], rs_send.at[kind, dx - 1], rs_recv.at[kind, dx - 1],
            (r, at_col(0, dx)),
        )

    def rs_start(kind):
        blocks = (2 * z, 2 * z + 1) if kind == OWN else (owned(3, kind - NEAR), owned(1, kind - NEAR))
        for cb in blocks:
            sbuf[cb] = acc[cb].astype(BF16)
        for dx in (1, 2, 3):
            rs_copy(kind, dx).start()

    def to_owner(src, rows, s_sem, cb, j):
        owner_yl, owner_x = cb // NX, lax.rem(cb, NX)
        rel = lax.rem(owner_yl + yl, 2)
        cp = remote(src, parts.at[j, rel, rows, :], s_sem, own_recv.at[j, rel], (r, owner_yl * NX + owner_x))
        return cp, jnp.logical_or(owner_x != x, owner_yl != yl)

    def own_copy(kind):
        cb, row = quarter(kind, x)
        return to_owner(stage.at[kind], pl.ds(0, tb), own_send.at[kind], cb, row // tb)

    def rs_collect(kind):
        cb, row = quarter(kind, x)
        total = acc[cb, pl.ds(row, tb), :]
        for dx in (1, 2, 3):
            rs_copy(kind, dx).wait_recv()
            total = total + rx[kind, dx - 1].astype(F32)
        stage[kind] = total.astype(BF16)
        cp, away = own_copy(kind)
        pl.when(away)(cp.start)

    def rs2_copy(p, dx):
        cb, row = quarter(FAR, lax.rem(x + dx, NX))
        return remote(
            sbuf.at[cb, pl.ds(pl.multiple_of(row + p * hb, hb), hb), :], rx.at[FAR, dx - 1, pl.ds(p * hb, hb), :],
            rs2_send.at[p, dx - 1], rs2_recv.at[p, dx - 1], (r, at_col(0, dx)),
        )

    def rs2_start(p):
        plane = lax.rem(z + 2, NZ)
        for q in range(4):
            row = q % 2 * tb + p * hb
            sbuf[2 * plane + q // 2, row:row + hb, :] = acc2[p, q * hb:(q + 1) * hb, :].astype(BF16)
        for dx in (1, 2, 3):
            rs2_copy(p, dx).start()

    def own2_copy(p):
        cb, row = quarter(FAR, x)
        part = pl.ds(p * hb, hb)
        return to_owner(stage.at[FAR, part, :], part, own_send.at[FAR + p], cb, row // tb)

    def rs2_collect(p):
        cb, row = quarter(FAR, x)
        row = lax.rem(cb, 2) * tb + row // 2
        total = acc2[p, pl.ds(pl.multiple_of(row, hb), hb), :]
        for dx in (1, 2, 3):
            rs2_copy(p, dx).wait_recv()
            total = total + rx[FAR, dx - 1, p * hb:(p + 1) * hb, :].astype(F32)
        stage[FAR, p * hb:(p + 1) * hb, :] = total.astype(BF16)
        cp, away = own2_copy(p)
        pl.when(away)(cp.start)

    def rs_finish():
        offset = lax.rem(c // 2 - z + NZ, NZ)
        beside = NEAR + lax.rem(lax.rem(c, 2) + yh, 2)
        mine = jnp.where(offset == 0, OWN, jnp.where(offset == 2, FAR, beside))

        def arrived(j, rel):
            here = parts.at[j, rel]
            remote(here, here, own_send.at[0], own_recv.at[j, rel], core_other).wait_recv()

        def keep():
            parts[0, 0] = stage[mine]

        pl.when(offset == 1)(lambda: arrived(0, 0))
        pl.when(offset != 1)(keep)
        for j in range(2):
            for rel in range(2):
                if j or rel:
                    arrived(j, rel)
            total = parts[j, 0].astype(F32) + parts[j, 1].astype(F32)
            gi_ref[j * tb:(j + 1) * tb, :] = total.astype(gi_ref.dtype)

    def near(i):
        for dz in (3, 1):
            got(dz, 0, 0, i)
            if i >= NA:
                push(dz, 0, i, y_other, dz, 1, 0)
            share(dz, 0, i)

    def other(i):
        got(0, 1, 0, i)
        if i < NA:
            push(0, 1, i, z_up, 3, 1, 0)
            push(0, 1, i, z_dn, 1, 1, 0)
        share(0, 1, i)

    def near_other(i):
        for dz in (3, 1):
            got(dz, 1, 0, i)
            share(dz, 1, i)
        if i < NA:
            relay(1, i, 0)

    def far(i, p):
        got2(0, 0, i, p)
        if i >= NA:
            push2(2, 0, i, p, y_other, 1, 0)
        push2(2, 0, i, p, core_other, 0, 1)

    def far_other(i, p):
        got2(1, 0, i, p)
        push2(2, 1, i, p, core_other, 1, 1)

    def forward_x():
        x_got(1, 0)
        for dx in (1, 2, 3):
            send_x(at_col(1, 0), (r, at_col(0, dx)), 3 + dx, x_recv.at[1, NX - dx])

    def clear(chunks):
        for i in chunks:
            dw_ref[i] = jnp.zeros_like(dw_ref[i])

    def before(n):
        if n == 0:
            acc[...] = jnp.zeros_like(acc)
            acc2[...] = jnp.zeros_like(acc2)
            near(0)
            forward_x()
            clear((0, 1))
            near(1)
            for cp in w_loads:
                cp.wait()
        if n == 1:
            other(0)
            near(2)
            other(1)
            clear((2, 3))
        if n == 2:
            near(3)
            other(2)
        if n == 3:
            near(4)
            other(3)
            clear((4, 5))
        if n == 6:
            near_other(1)
        if n == 7:
            other(4)
            other(5)
        if n == 8:
            near_other(2)
        if n == 9:
            near_other(3)
            for dy in range(2):
                for i in range(NA):
                    relay(dy, i, 1)
            near_other(4)
        if n == 12:
            far_other(2, 0)
            far_other(3, 0)
        if n == 13:
            far_other(4, 0)
            far_other(5, 0)
        if n == 15:
            far_other(0, 1)
            far_other(1, 1)
        if n == 16:
            far_other(2, 1)
            far_other(3, 1)
        if MM1[n] is not None:
            sib(*MM1[n])
        if MM1H[n] is not None:
            sib2(*MM1H[n])
        if n == 13:
            rs_collect(NEAR)
            rs_collect(OWN)
        if n == 15:
            rs_collect(CROSS)
        if n == 19:
            rs2_collect(0)

    def between(n):
        if n == 3:
            near(5)
            for i in (4, 5):
                for p in range(2):
                    relay(0, i, p)
            for i in range(NA):
                relay(0, i, 0)
            for dyl in range(2):
                for dx in (1, 2, 3):
                    x_got(dyl, dx)
            for cb in range(2 * NZ):
                xt[cb] = xbuf[cb].T
        if n == 4:
            rs_start(NEAR)
            near_other(0)
        if n == 8:
            rs_start(OWN)
        if n == 10:
            near_other(5)
            for p in range(2):
                far(4, p)
                far(5, p)
        if n == 11:
            rs_start(CROSS)
            for i in range(NA):
                far(i, 0)
            far_other(0, 0)
            far_other(1, 0)
        if n == 13:
            for i in range(NA):
                far(i, 1)
            far_other(4, 1)
            far_other(5, 1)
        if n == 14:
            rs2_start(0)
        if n == 17:
            rs2_start(1)

    @pl.loop(0, STEPS)
    def _(step):
        choose(step, before, 0, STEPS)
        pl.when(busy(MM1, step))(lambda: mm1(step))
        pl.when(busy(MM1H, step))(lambda: mm1h(step))
        choose(step, between, 0, STEPS)
        pl.when(busy(MM2, step))(lambda: mm2(step))

    rs2_collect(1)
    rs_finish()

    assert n_sent[0] == N_SENDS and n_sent2[0] == N_SENDS2
    for n in range(N_SENDS):
        here = block(0, 0, 0, 0)
        remote(here, here, send_sem.at[n], recv_sem.at[0, 0, 0, 0], core_other).wait_send()
    for n in range(N_SENDS2):
        here = half(0, 0, 0, 0, 0)
        remote(here, here, send_sem.at[N_SENDS + n], recv_sem.at[0, 0, 0, 0], core_other).wait_send()
    for n in range(7):
        remote(xbuf.at[c], xbuf.at[c], x_send.at[n], x_recv.at[0, 0], core_other).wait_send()
    last = []
    for kind in (OWN, NEAR, CROSS):
        for dx in (1, 2, 3):
            rs_copy(kind, dx).wait_send()
        last.append(own_copy(kind))
    for p in range(2):
        for dx in (1, 2, 3):
            rs2_copy(p, dx).wait_send()
        last.append(own2_copy(p))
    for cp, away in last:
        pl.when(away)(cp.wait_send)


N_SENDS = (12 + 8) + (6 + 4) + 36
N_SENDS2 = 20 + 4 + 24


def out_kernel(gi_ref, dw_ref, gi_out, dw_out, buf, sem):
    cw = dw_ref.shape[2]
    gi_copy = pltpu.make_async_copy(gi_ref, gi_out, sem.at[NCH])
    gi_copy.start()
    copies = []
    for i in range(NCH):
        buf[i] = dw_ref[i].astype(buf.dtype)
        cp = pltpu.make_async_copy(buf.at[i], dw_out.at[:, pl.ds(i * cw, cw)], sem.at[i])
        cp.start()
        copies.append(cp)
    for cp in copies:
        cp.wait()
    gi_copy.wait()


def body(grad_hidden, pre_act, inputs, weight):
    tb, ft = grad_hidden.shape
    ob, dt = inputs.shape
    cw = ft // NCH
    hbm = pl.BlockSpec(memory_space=pltpu.HBM)
    vmem = pl.BlockSpec(memory_space=pltpu.VMEM)
    dma = pltpu.SemaphoreType.DMA
    gi, dw = pl.pallas_call(
        main_kernel,
        out_shape=(pltpu.VMEM((ob, dt), BF16), pltpu.VMEM((NCH, dt, cw), F32)),
        in_specs=[hbm] * 4,
        out_specs=(vmem, vmem),
        scratch_shapes=[
            pltpu.VMEM((NCH, tb, cw), BF16),
            pltpu.VMEM((NCH, tb, cw), BF16),
            pltpu.VMEM((NCH, 8, ob, cw), BF16),
            pltpu.VMEM((NCH, dt, cw), BF16),
            pltpu.VMEM((8, ob, dt), BF16),
            pltpu.VMEM((8, dt, ob), BF16),
            pltpu.VMEM((8, ob, dt), F32),
            pltpu.VMEM((2, ob, dt), F32),
            pltpu.VMEM((8, ob, dt), BF16),
            pltpu.VMEM((4, NX - 1, tb, dt), BF16),
            pltpu.VMEM((4, tb, dt), BF16),
            pltpu.VMEM((2, 2, tb, dt), BF16),
            dma((2, NCH)),
            dma((NCH,)),
            dma,
            dma((N_SENDS + N_SENDS2,)),
            dma((2, 2, NZ, NCH)),
            dma((2, 2, NCH, 2)),
            dma((7,)),
            dma((2, NX)),
            dma((3, NX - 1)),
            dma((3, NX - 1)),
            dma((2, NX - 1)),
            dma((2, NX - 1)),
            dma((5,)),
            dma((2, 2)),
        ],
        compiler_params=pltpu.CompilerParams(
            collective_id=0, has_side_effects=True, vmem_limit_bytes=44 * 2**20
        ),
        name="gather_and_multiply",
    )(grad_hidden, pre_act, inputs, weight)
    return pl.pallas_call(
        out_kernel,
        out_shape=(
            jax.ShapeDtypeStruct((ob, dt), BF16),
            jax.ShapeDtypeStruct((dt, ft), BF16),
        ),
        in_specs=[vmem, vmem],
        out_specs=(hbm, hbm),
        scratch_shapes=[pltpu.VMEM((NCH, dt, cw), BF16), dma((NCH + 1,))],
        compiler_params=pltpu.CompilerParams(vmem_limit_bytes=20 * 2**20),
        name="round_and_write",
    )(gi, dw)


def solution(mesh):
    return jax.shard_map(
        body,
        mesh=mesh,
        in_specs=(P("row", "col"), P("row", "col"), P("col", "row"), P("row", "col")),
        out_specs=(P("col", "row"), P("row", "col")),
        check_vma=False,
    )
```

```python
import math

import jax
import jax.numpy as jnp
from jax import lax
from jax.experimental import pallas as pl
from jax.experimental.pallas import tpu as pltpu
from jax.sharding import PartitionSpec as P

NZ = 4
NX = 4
NCH = 6
NA = 4
GROUPS = ((0, 1), (2, 3), (4, 5))
OWN, NEAR, CROSS, FAR = range(4)
STEP = (
    ((NEAR, 0), None, None),
    ((OWN, 0), None, None),
    ((NEAR, 1), None, None),
    ((OWN, 1), None, (OWN, 0)),
    ((NEAR, 2), None, (NEAR, 0)),
    (None, None, (OWN, 1)),
    (None, None, (NEAR, 1)),
    ((CROSS, 0), None, (NEAR, 2)),
    ((OWN, 2), None, (OWN, 2)),
    (None, None, (CROSS, 0)),
    ((CROSS, 1), None, (CROSS, 1)),
    ((CROSS, 2), None, (CROSS, 2)),
    (None, (0, 0), None),
    (None, (0, 1), None),
    (None, (0, 2), None),
    (None, (1, 2), None),
    (None, (1, 0), None),
    (None, (1, 1), None),
    (None, None, (FAR, 2)),
    (None, None, (FAR, 0)),
    (None, None, (FAR, 1)),
)
MM1, MM1H, MM2 = zip(*STEP)
STEPS = len(STEP)
NT = (((1,), (1,)), ((), ()))
NN = (((1,), (0,)), ((), ()))
BF16 = jnp.bfloat16
F32 = jnp.float32


def gelu_grad(value):
    coeff = math.sqrt(2.0 / math.pi)
    inner = coeff * (value + 0.044715 * value * value * value)
    tanh_value = jnp.tanh(inner)
    return 0.5 * (1.0 + tanh_value) + 0.5 * value * (1.0 - tanh_value * tanh_value) * coeff * (
        1.0 + 3.0 * 0.044715 * value * value
    )


def main_kernel(
    g_hbm, v_hbm, x_hbm, w_hbm,
    gi_ref, dw_ref,
    gvbuf, panel, wbuf, xbuf, xt, acc, acc2, sbuf, rx, stage, parts,
    load_sem, w_sem, x_own_sem, send_sem, recv_sem, far_sem, core_sem, core2_sem, x_send, x_recv, rs_send, rs_recv,
    rs2_recv, own_send, own_recv,
):
    r = lax.axis_index("row")
    c = lax.axis_index("col")
    z, yh, k = r // 4, (r // 2) % 2, r % 2
    yl, x = c // NX, c % NX
    tb = g_hbm.shape[0]
    cw = panel.shape[3]
    ob = x_hbm.shape[0]

    def at_row(dz, dy, dk):
        return lax.rem(z + dz, NZ) * 4 + lax.rem(yh + dy, 2) * 2 + lax.rem(k + dk, 2)

    def at_col(dyl, dx):
        return lax.rem(yl + dyl, 2) * NX + lax.rem(x + dx, NX)

    z_up, z_dn = (at_row(1, 0, 0), c), (at_row(3, 0, 0), c)
    y_other, core_other = (at_row(0, 1, 0), c), (at_row(0, 0, 1), c)

    x_own = pltpu.make_async_copy(x_hbm, xbuf.at[c], x_own_sem)
    x_own.start()
    for i in range(NCH):
        cols = pl.ds(i * cw, cw)
        for n, src in enumerate((g_hbm, v_hbm)):
            pltpu.make_async_copy(src.at[:, cols], gvbuf.at[i, n], load_sem.at[min(i, 1)]).start()
    barrier = pltpu.get_barrier_semaphore()
    partners = [z_up, z_dn, y_other, core_other, (r, at_col(1, 0))]
    partners += [(r, at_col(0, dx)) for dx in (1, 2, 3)]
    for partner in partners:
        pl.semaphore_signal(barrier, inc=1, device_id=partner, device_id_type=pl.DeviceIdType.MESH)

    def grad_pre(i):
        if i < 2:
            part = gvbuf.at[pl.ds(0, 1) if i == 0 else pl.ds(1, NCH - 1)]
            pltpu.make_async_copy(part, part, load_sem.at[i]).wait()
        value = gvbuf[i, 0].astype(F32) * gelu_grad(gvbuf[i, 1].astype(F32))
        panel[i, 2 * z + yh, pl.ds(pl.multiple_of(k * tb, tb), tb), :] = value.astype(BF16)

    grad_pre(0)
    pl.semaphore_wait(barrier, len(partners))

    hb = tb // 2
    n_sent = [0]
    n_sent2 = [0]

    def remote(src, dst, s_sem, r_sem, target):
        return pltpu.make_async_remote_copy(
            src_ref=src, dst_ref=dst, send_sem=s_sem, recv_sem=r_sem,
            device_id=target, device_id_type=pl.DeviceIdType.MESH,
        )

    def owned(dz, dy):
        return 2 * lax.rem(z + dz, NZ) + lax.rem(yh + dy, 2)

    def block(dz, dy, dk, i):
        rows = pl.ds(pl.multiple_of(lax.rem(k + dk, 2) * tb, tb), tb)
        return panel.at[i, owned(dz, dy), rows, :]

    def half(dz, dy, dk, i, p):
        rows = pl.ds(pl.multiple_of(lax.rem(k + dk, 2) * tb + p * hb, hb), hb)
        return panel.at[i, owned(dz, dy), rows, :]

    def push(dz, dy, i, target, sem):
        here = block(dz, dy, 0, i)
        s_sem = send_sem.at[0 if n_sent[0] < FIRST_SENDS else 1]
        remote(here, here, s_sem, sem, target).start()
        n_sent[0] += 1

    def push2(dz, dy, i, p, target, sem):
        here = half(dz, dy, 0, i, p)
        remote(here, here, send_sem.at[1], sem, target).start()
        n_sent2[0] += 1

    def took(ref, sem):
        remote(ref, ref, send_sem.at[0], sem, core_other).wait_recv()

    def blocks_of(n, m, rows):
        return panel.at[pl.ds(0, n), pl.ds(0, m), pl.ds(0, rows), :]

    def share(dz, dy, i):
        kind = OWN if dz == 0 else NEAR + dy
        push(dz, dy, i, core_other, core_sem.at[kind, i // 2])

    def share2(dy, i, p):
        push2(2, dy, i, p, core_other, core2_sem.at[p, i // 2])

    def far_slot(dy, i, p):
        if dy:
            return far_sem.at[3 + 3 * p + i // 2]
        return far_sem.at[2 if i >= NA else p]

    def relay(dy, i, p):
        if i % 2 == 0:
            push2(3, dy, i, p, z_up, far_slot(dy, i, p))
        else:
            push2(1, dy, i, p, z_dn, far_slot(dy, i, p))

    def send_x(cb, target, rs):
        remote(xbuf.at[cb], xbuf.at[cb], x_send, rs, target).start()

    x_own.wait()
    send_x(c, (r, at_col(1, 0)), x_recv.at[0])
    for dx in (1, 2, 3):
        send_x(c, (r, at_col(0, dx)), x_recv.at[1])

    for i in range(NCH):
        if i:
            grad_pre(i)
        push(0, 0, i, z_up, recv_sem.at[0, i])
        push(0, 0, i, z_dn, recv_sem.at[0, i])
        push(0, 0, i, y_other, recv_sem.at[2, i])
        share(0, 0, i)

    for i in range(NCH):
        cols = pl.ds(i * cw, cw)
        cp = pltpu.make_async_copy(w_hbm.at[:, cols], wbuf.at[i], w_sem)
        cp.start()

    def packed(values, step):
        def word(part):
            w = sum(v << (2 * n) for n, v in enumerate(part))
            return jnp.int32(w - (1 << 32) if w >> 31 else w)

        w = jnp.where(step < 16, word(values[:16]), word(values[16:]))
        return lax.shift_right_arithmetic(w, 2 * lax.rem(step, 16)) & 3

    def unit(units, step):
        return packed([u[0] if u else 0 for u in units], step), packed([u[1] if u else 0 for u in units], step)

    def pair(kind):
        def of(own, near, cross, far):
            return jnp.where(kind < 2, jnp.where(kind == 0, own, near), jnp.where(kind == 2, cross, far))

        first = of(2 * z, owned(3, 0), owned(3, 1), 2 * lax.rem(z + 2, NZ))
        second = of(2 * z + 1, owned(1, 0), owned(1, 1), 2 * lax.rem(z + 2, NZ) + 1)
        return first, second

    def busy(units, step):
        return packed([0 if u is None else 1 for u in units], step) == 1

    def choose(step, what, lo, hi):
        if hi - lo == 1:
            what(lo)
        else:
            mid = (lo + hi) // 2
            lax.cond(
                step < mid, lambda: choose(step, what, lo, mid), lambda: choose(step, what, mid, hi)
            )

    def mm1(step):
        kind, group = unit(MM1, step)
        blocks = pair(kind)
        term = None
        for j in range(2):
            i = 2 * group + j
            left = jnp.concatenate([panel[i, cb] for cb in blocks], axis=0)
            d = lax.dot_general(left, wbuf[i], NT, preferred_element_type=F32)
            term = d if term is None else term + d
        for n, cb in enumerate(blocks):
            acc[cb] = acc[cb] + term[n * ob:(n + 1) * ob]

    def mm1h(step):
        p, group = unit(MM1H, step)
        plane = lax.rem(z + 2, NZ)
        term = None
        for j in range(2):
            i = 2 * group + j
            rows = [
                panel[i, 2 * plane + q // 2, pl.ds(pl.multiple_of(q % 2 * tb + p * hb, hb), hb), :] for q in range(4)
            ]
            d = lax.dot_general(jnp.concatenate(rows, axis=0), wbuf[i], NT, preferred_element_type=F32)
            term = d if term is None else term + d
        acc2[p] = acc2[p] + term

    def mm2(step):
        kind, group = unit(MM2, step)
        blocks = pair(kind)
        left = jnp.concatenate([xt[cb] for cb in blocks], axis=1)
        for j in range(2):
            i = 2 * group + j
            right = jnp.concatenate([panel[i, cb] for cb in blocks], axis=0)
            d = lax.dot_general(left, right, NN, preferred_element_type=F32)
            dw_ref[i] = dw_ref[i] + d

    def sib(kind, group):
        took(blocks_of(2, 2, tb), core_sem.at[kind, group])

    def sib2(p, group):
        took(blocks_of(2, 2, hb), core2_sem.at[p, group])

    def quarter(kind, xc):
        near = xc // 2 == lax.rem(z + (kind in (NEAR, CROSS)), 2)
        h = jnp.where(near, lax.rem(xc, 2), 1 - lax.rem(xc, 2))
        row = pl.multiple_of(jnp.where(near, 0, tb), tb)
        if kind in (OWN, FAR):
            return 2 * lax.rem(z + kind // FAR * 2, NZ) + h, row
        dy = kind - NEAR
        return jnp.where(h == lax.rem(yh + dy, 2), owned(3, dy), owned(1, dy)), row

    def rs_copy(kind, dx):
        cb, row = quarter(kind, lax.rem(x + dx, NX))
        return remote(
            sbuf.at[cb, pl.ds(row, tb), :], rx.at[kind, dx - 1], rs_send, rs_recv.at[kind],
            (r, at_col(0, dx)),
        )

    def rs_start(kind):
        blocks = (2 * z, 2 * z + 1) if kind == OWN else (owned(3, kind - NEAR), owned(1, kind - NEAR))
        for cb in blocks:
            sbuf[cb] = acc[cb].astype(BF16)
        for dx in (1, 2, 3):
            rs_copy(kind, dx).start()

    def to_owner(src, rows, s_sem, cb, j):
        owner_yl, owner_x = cb // NX, lax.rem(cb, NX)
        rel = lax.rem(owner_yl + yl, 2)
        cp = remote(src, parts.at[j, rel, rows, :], s_sem, own_recv.at[j, rel], (r, owner_yl * NX + owner_x))
        return cp, jnp.logical_or(owner_x != x, owner_yl != yl)

    def own_copy(kind):
        cb, row = quarter(kind, x)
        return to_owner(stage.at[kind], pl.ds(0, tb), own_send.at[kind], cb, row // tb)

    def rs_collect(kind):
        cb, row = quarter(kind, x)
        total = acc[cb, pl.ds(row, tb), :]
        took(rx.at[kind], rs_recv.at[kind])
        for dx in (1, 2, 3):
            total = total + rx[kind, dx - 1].astype(F32)
        stage[kind] = total.astype(BF16)
        cp, away = own_copy(kind)
        pl.when(away)(cp.start)

    def rs2_copy(p, dx):
        cb, row = quarter(FAR, lax.rem(x + dx, NX))
        return remote(
            sbuf.at[cb, pl.ds(pl.multiple_of(row + p * hb, hb), hb), :], rx.at[FAR, dx - 1, pl.ds(p * hb, hb), :],
            rs_send, rs2_recv.at[p], (r, at_col(0, dx)),
        )

    def rs2_start(p):
        plane = lax.rem(z + 2, NZ)
        for q in range(4):
            row = q % 2 * tb + p * hb
            sbuf[2 * plane + q // 2, row:row + hb, :] = acc2[p, q * hb:(q + 1) * hb, :].astype(BF16)
        for dx in (1, 2, 3):
            rs2_copy(p, dx).start()

    def own2_copy(p):
        cb, row = quarter(FAR, x)
        part = pl.ds(p * hb, hb)
        return to_owner(stage.at[FAR, part, :], part, own_send.at[FAR + p], cb, row // tb)

    def rs2_collect(p):
        cb, row = quarter(FAR, x)
        row = lax.rem(cb, 2) * tb + row // 2
        total = acc2[p, pl.ds(pl.multiple_of(row, hb), hb), :]
        took(rx.at[FAR, :, pl.ds(p * hb, hb), :], rs2_recv.at[p])
        for dx in (1, 2, 3):
            total = total + rx[FAR, dx - 1, p * hb:(p + 1) * hb, :].astype(F32)
        stage[FAR, p * hb:(p + 1) * hb, :] = total.astype(BF16)
        cp, away = own2_copy(p)
        pl.when(away)(cp.start)

    def rs_finish():
        offset = lax.rem(c // 2 - z + NZ, NZ)
        beside = NEAR + lax.rem(lax.rem(c, 2) + yh, 2)
        mine = jnp.where(offset == 0, OWN, jnp.where(offset == 2, FAR, beside))

        def arrived(j, rel):
            here = parts.at[j, rel]
            remote(here, here, own_send.at[0], own_recv.at[j, rel], core_other).wait_recv()

        def keep():
            parts[0, 0] = stage[mine]

        pl.when(offset == 1)(lambda: arrived(0, 0))
        pl.when(offset != 1)(keep)
        for j in range(2):
            for rel in range(2):
                if j or rel:
                    arrived(j, rel)
            total = parts[j, 0].astype(F32) + parts[j, 1].astype(F32)
            gi_ref[j * tb:(j + 1) * tb, :] = total.astype(gi_ref.dtype)

    def near(i):
        took(blocks_of(1, 2, tb), recv_sem.at[0, i])
        for dz in (3, 1):
            if i >= NA:
                push(dz, 0, i, y_other, recv_sem.at[1, i])
            share(dz, 0, i)

    def other(i):
        took(blocks_of(1, 1, tb), recv_sem.at[2, i])
        if i < NA:
            push(0, 1, i, z_up, recv_sem.at[1, i])
            push(0, 1, i, z_dn, recv_sem.at[1, i])
        share(0, 1, i)

    def near_other(i):
        took(blocks_of(1, 2, tb), recv_sem.at[1, i])
        for dz in (3, 1):
            share(dz, 1, i)
        if i < NA:
            relay(1, i, 0)

    def far(chunks, halves):
        took(blocks_of(1, len(chunks) * len(halves), hb), far_slot(0, chunks[0], halves[0]))
        for p in halves:
            for i in chunks:
                if i >= NA:
                    push2(2, 0, i, p, y_other, far_slot(1, i, p))
                share2(0, i, p)

    def far_other(group, p):
        took(blocks_of(1, 2, hb), far_slot(1, 2 * group, p))
        for i in GROUPS[group]:
            share2(1, i, p)

    def forward_x():
        took(xbuf.at[pl.ds(0, 1)], x_recv.at[0])
        for dx in (1, 2, 3):
            send_x(at_col(1, 0), (r, at_col(0, dx)), x_recv.at[1])

    def clear(chunks):
        for i in chunks:
            dw_ref[i] = jnp.zeros_like(dw_ref[i])

    def before(n):
        if n == 0:
            acc[...] = jnp.zeros_like(acc)
            acc2[...] = jnp.zeros_like(acc2)
            near(0)
            forward_x()
            clear((0, 1))
            near(1)
            pltpu.make_async_copy(wbuf, wbuf, w_sem).wait()
        if n == 1:
            other(0)
            near(2)
            other(1)
            clear((2, 3))
        if n == 2:
            near(3)
            other(2)
        if n == 3:
            near(4)
            other(3)
            clear((4, 5))
        if n == 6:
            near_other(1)
        if n == 7:
            other(4)
            other(5)
        if n == 8:
            near_other(2)
        if n == 9:
            near_other(3)
            for dy in range(2):
                for i in range(NA):
                    relay(dy, i, 1)
            near_other(4)
        if n == 12:
            far_other(1, 0)
        if n == 13:
            far_other(2, 0)
        if n == 15:
            far_other(0, 1)
        if n == 16:
            far_other(1, 1)
        if MM1[n] is not None:
            sib(*MM1[n])
        if MM1H[n] is not None:
            sib2(*MM1H[n])
        if n == 12:
            rs_collect(NEAR)
        if n == 12:
            rs_collect(OWN)
        if n == 15:
            rs_collect(CROSS)
        if n == 19:
            rs2_collect(0)

    def between(n):
        if n == 3:
            near(5)
            for i in (4, 5):
                for p in range(2):
                    relay(0, i, p)
            for i in range(NA):
                relay(0, i, 0)
            took(xbuf.at[pl.ds(0, 6)], x_recv.at[1])
            for cb in range(2 * NZ):
                xt[cb] = xbuf[cb].T
        if n == 4:
            rs_start(NEAR)
            near_other(0)
        if n == 8:
            rs_start(OWN)
        if n == 10:
            near_other(5)
            far((4, 5), (0, 1))
        if n == 11:
            rs_start(CROSS)
            far((0, 1, 2, 3), (0,))
            far_other(0, 0)
        if n == 13:
            far((0, 1, 2, 3), (1,))
            far_other(2, 1)
        if n == 14:
            rs2_start(0)
        if n == 17:
            rs2_start(1)

    @pl.loop(0, STEPS)
    def _(step):
        choose(step, before, 0, STEPS)
        pl.when(busy(MM1, step))(lambda: mm1(step))
        pl.when(busy(MM1H, step))(lambda: mm1h(step))
        choose(step, between, 0, STEPS)
        pl.when(busy(MM2, step))(lambda: mm2(step))

    rs2_collect(1)
    rs_finish()

    assert n_sent[0] == N_SENDS and n_sent2[0] == N_SENDS2
    rest = 2 * (N_SENDS - FIRST_SENDS) + N_SENDS2
    for sem, ref in (
        (send_sem.at[0], blocks_of(NCH, FIRST_SENDS // NCH, tb)),
        (send_sem.at[1], blocks_of(NCH, rest // 2 // NCH, tb)),
        (x_send, xbuf.at[pl.ds(0, 7)]),
        (rs_send, rx),
    ):
        remote(ref, ref, sem, recv_sem.at[0, 0], core_other).wait_send()
    last = [own_copy(kind) for kind in (OWN, NEAR, CROSS)] + [own2_copy(p) for p in range(2)]
    for cp, away in last:
        pl.when(away)(cp.wait_send)


N_SENDS = (12 + 8) + (6 + 4) + 36
N_SENDS2 = 20 + 4 + 24
FIRST_SENDS = 48


def out_kernel(gi_ref, dw_ref, gi_out, dw_out, buf, sem):
    cw = dw_ref.shape[2]
    gi_copy = pltpu.make_async_copy(gi_ref, gi_out, sem.at[NCH])
    gi_copy.start()
    copies = []
    for i in range(NCH):
        buf[i] = dw_ref[i].astype(buf.dtype)
        cp = pltpu.make_async_copy(buf.at[i], dw_out.at[:, pl.ds(i * cw, cw)], sem.at[i])
        cp.start()
        copies.append(cp)
    for cp in copies:
        cp.wait()
    gi_copy.wait()


def body(grad_hidden, pre_act, inputs, weight):
    tb, ft = grad_hidden.shape
    ob, dt = inputs.shape
    cw = ft // NCH
    hbm = pl.BlockSpec(memory_space=pltpu.HBM)
    vmem = pl.BlockSpec(memory_space=pltpu.VMEM)
    dma = pltpu.SemaphoreType.DMA
    gi, dw = pl.pallas_call(
        main_kernel,
        out_shape=(pltpu.VMEM((ob, dt), BF16), pltpu.VMEM((NCH, dt, cw), F32)),
        in_specs=[hbm] * 4,
        out_specs=(vmem, vmem),
        scratch_shapes=[
            pltpu.VMEM((NCH, 2, tb, cw), BF16),
            pltpu.VMEM((NCH, 8, ob, cw), BF16),
            pltpu.VMEM((NCH, dt, cw), BF16),
            pltpu.VMEM((8, ob, dt), BF16),
            pltpu.VMEM((8, dt, ob), BF16),
            pltpu.VMEM((8, ob, dt), F32),
            pltpu.VMEM((2, ob, dt), F32),
            pltpu.VMEM((8, ob, dt), BF16),
            pltpu.VMEM((4, NX - 1, tb, dt), BF16),
            pltpu.VMEM((4, tb, dt), BF16),
            pltpu.VMEM((2, 2, tb, dt), BF16),
            dma((2,)),
            dma,
            dma,
            dma((2,)),
            dma((3, NCH)),
            dma((9,)),
            dma((3, 3)),
            dma((2, 3)),
            dma,
            dma((2,)),
            dma,
            dma((3,)),
            dma((2,)),
            dma((5,)),
            dma((2, 2)),
        ],
        compiler_params=pltpu.CompilerParams(
            collective_id=0, has_side_effects=True, vmem_limit_bytes=44 * 2**20
        ),
        name="gather_and_multiply",
    )(grad_hidden, pre_act, inputs, weight)
    return pl.pallas_call(
        out_kernel,
        out_shape=(
            jax.ShapeDtypeStruct((ob, dt), BF16),
            jax.ShapeDtypeStruct((dt, ft), BF16),
        ),
        in_specs=[vmem, vmem],
        out_specs=(hbm, hbm),
        scratch_shapes=[pltpu.VMEM((NCH, dt, cw), BF16), dma((NCH + 1,))],
        compiler_params=pltpu.CompilerParams(vmem_limit_bytes=20 * 2**20),
        name="round_and_write",
    )(gi, dw)


def solution(mesh):
    return jax.shard_map(
        body,
        mesh=mesh,
        in_specs=(P("row", "col"), P("row", "col"), P("col", "row"), P("row", "col")),
        out_specs=(P("col", "row"), P("row", "col")),
        check_vma=False,
    )
```

```python
import math

import jax
import jax.numpy as jnp
from jax import lax
from jax.experimental import pallas as pl
from jax.experimental.pallas import tpu as pltpu
from jax.sharding import PartitionSpec as P

NZ = 4
NX = 4
NCH = 6
NA = 4
GROUPS = ((0, 1), (2, 3), (4, 5))
OWN, NEAR, CROSS, FAR = range(4)
STEP = (
    ((NEAR, 0), None, None),
    ((OWN, 0), None, None),
    ((NEAR, 1), None, None),
    ((OWN, 1), None, (OWN, 0)),
    ((NEAR, 2), None, (NEAR, 0)),
    (None, None, (OWN, 1)),
    (None, None, (NEAR, 1)),
    ((CROSS, 0), None, (NEAR, 2)),
    ((OWN, 2), None, (OWN, 2)),
    (None, None, (CROSS, 0)),
    ((CROSS, 1), None, (CROSS, 1)),
    ((CROSS, 2), None, (CROSS, 2)),
    (None, (0, 0), None),
    (None, (0, 1), None),
    (None, (0, 2), None),
    (None, (1, 2), None),
    (None, (1, 0), None),
    (None, (1, 1), None),
    (None, None, (FAR, 2)),
    (None, None, (FAR, 0)),
    (None, None, (FAR, 1)),
)
MM1, MM1H, MM2 = zip(*STEP)
STEPS = len(STEP)
NT = (((1,), (1,)), ((), ()))
NN = (((1,), (0,)), ((), ()))
BF16 = jnp.bfloat16
F32 = jnp.float32


def gelu_grad(value):
    coeff = math.sqrt(2.0 / math.pi)
    inner = coeff * (value + 0.044715 * value * value * value)
    tanh_value = jnp.tanh(inner)
    return 0.5 * (1.0 + tanh_value) + 0.5 * value * (1.0 - tanh_value * tanh_value) * coeff * (
        1.0 + 3.0 * 0.044715 * value * value
    )


def main_kernel(
    g_hbm, v_hbm, x_hbm, w_hbm,
    gi_ref, dw_ref,
    gvbuf, panel, wbuf, xbuf, xt, acc, acc2, sbuf, rx, stage, parts,
    load_sem, w_sem, x_own_sem, send_sem, recv_sem, far_sem, core_sem, core2_sem, x_send, x_recv, rs_send, rs_recv,
    rs2_recv, own_send, own_recv,
):
    r = lax.axis_index("row")
    c = lax.axis_index("col")
    z, yh, k = r // 4, (r // 2) % 2, r % 2
    yl, x = c // NX, c % NX
    tb = g_hbm.shape[0]
    cw = panel.shape[3]
    ob = x_hbm.shape[0]

    def at_row(dz, dy, dk):
        return lax.rem(z + dz, NZ) * 4 + lax.rem(yh + dy, 2) * 2 + lax.rem(k + dk, 2)

    def at_col(dyl, dx):
        return lax.rem(yl + dyl, 2) * NX + lax.rem(x + dx, NX)

    z_up, z_dn = (at_row(1, 0, 0), c), (at_row(3, 0, 0), c)
    y_other, core_other = (at_row(0, 1, 0), c), (at_row(0, 0, 1), c)

    x_own = pltpu.make_async_copy(x_hbm, xbuf.at[c], x_own_sem)
    x_own.start()
    for i in range(NCH):
        cols = pl.ds(i * cw, cw)
        for n, src in enumerate((g_hbm, v_hbm)):
            pltpu.make_async_copy(src.at[:, cols], gvbuf.at[i, n], load_sem.at[min(i, 1)]).start()
    barrier = pltpu.get_barrier_semaphore()
    partners = [z_up, z_dn, y_other, core_other, (r, at_col(1, 0))]
    partners += [(r, at_col(0, dx)) for dx in (1, 2, 3)]
    for partner in partners:
        pl.semaphore_signal(barrier, inc=1, device_id=partner, device_id_type=pl.DeviceIdType.MESH)

    def grad_pre(i):
        if i < 2:
            part = gvbuf.at[pl.ds(0, 1) if i == 0 else pl.ds(1, NCH - 1)]
            pltpu.make_async_copy(part, part, load_sem.at[i]).wait()
        value = gvbuf[i, 0].astype(F32) * gelu_grad(gvbuf[i, 1].astype(F32))
        panel[i, 2 * z + yh, pl.ds(pl.multiple_of(k * tb, tb), tb), :] = value.astype(BF16)

    grad_pre(0)
    pl.semaphore_wait(barrier, len(partners))

    hb = tb // 2
    n_sent = [0]
    n_sent2 = [0]

    def remote(src, dst, s_sem, r_sem, target):
        return pltpu.make_async_remote_copy(
            src_ref=src, dst_ref=dst, send_sem=s_sem, recv_sem=r_sem,
            device_id=target, device_id_type=pl.DeviceIdType.MESH,
        )

    def owned(dz, dy):
        return 2 * lax.rem(z + dz, NZ) + lax.rem(yh + dy, 2)

    def block(dz, dy, dk, i):
        rows = pl.ds(pl.multiple_of(lax.rem(k + dk, 2) * tb, tb), tb)
        return panel.at[i, owned(dz, dy), rows, :]

    def half(dz, dy, dk, i, p):
        rows = pl.ds(pl.multiple_of(lax.rem(k + dk, 2) * tb + p * hb, hb), hb)
        return panel.at[i, owned(dz, dy), rows, :]

    def push(dz, dy, i, target, sem):
        here = block(dz, dy, 0, i)
        s_sem = send_sem.at[0 if n_sent[0] < FIRST_SENDS else 1]
        remote(here, here, s_sem, sem, target).start()
        n_sent[0] += 1

    def push2(dz, dy, i, p, target, sem):
        here = half(dz, dy, 0, i, p)
        remote(here, here, send_sem.at[1], sem, target).start()
        n_sent2[0] += 1

    def took(ref, sem):
        remote(ref, ref, send_sem.at[0], sem, core_other).wait_recv()

    def blocks_of(n, m, rows):
        return panel.at[pl.ds(0, n), pl.ds(0, m), pl.ds(0, rows), :]

    def share(dz, dy, i):
        kind = OWN if dz == 0 else NEAR + dy
        push(dz, dy, i, core_other, core_sem.at[kind, i // 2])

    def share2(dy, i, p):
        push2(2, dy, i, p, core_other, core2_sem.at[p, i // 2])

    def far_slot(dy, i, p):
        if dy:
            return far_sem.at[3 + 3 * p + i // 2]
        return far_sem.at[2 if i >= NA else p]

    def relay(dy, i, p):
        if i % 2 == 0:
            push2(3, dy, i, p, z_up, far_slot(dy, i, p))
        else:
            push2(1, dy, i, p, z_dn, far_slot(dy, i, p))

    def send_x(cb, target, rs):
        remote(xbuf.at[cb], xbuf.at[cb], x_send, rs, target).start()

    for i in range(NCH):
        if i:
            grad_pre(i)
        push(0, 0, i, z_up, recv_sem.at[0, i])
        push(0, 0, i, z_dn, recv_sem.at[0, i])
        if i == 0:
            x_own.wait()
            send_x(c, (r, at_col(1, 0)), x_recv.at[0])
            for dx in (1, 2, 3):
                send_x(c, (r, at_col(0, dx)), x_recv.at[1])
        push(0, 0, i, y_other, recv_sem.at[2, i])
        share(0, 0, i)

    for i in range(NCH):
        cols = pl.ds(i * cw, cw)
        cp = pltpu.make_async_copy(w_hbm.at[:, cols], wbuf.at[i], w_sem)
        cp.start()

    def packed(values, step):
        def word(part):
            w = sum(v << (2 * n) for n, v in enumerate(part))
            return jnp.int32(w - (1 << 32) if w >> 31 else w)

        w = jnp.where(step < 16, word(values[:16]), word(values[16:]))
        return lax.shift_right_arithmetic(w, 2 * lax.rem(step, 16)) & 3

    def unit(units, step):
        return packed([u[0] if u else 0 for u in units], step), packed([u[1] if u else 0 for u in units], step)

    def pair(kind):
        def of(own, near, cross, far):
            return jnp.where(kind < 2, jnp.where(kind == 0, own, near), jnp.where(kind == 2, cross, far))

        first = of(2 * z, owned(3, 0), owned(3, 1), 2 * lax.rem(z + 2, NZ))
        second = of(2 * z + 1, owned(1, 0), owned(1, 1), 2 * lax.rem(z + 2, NZ) + 1)
        return first, second

    def busy(units, step):
        return packed([0 if u is None else 1 for u in units], step) == 1

    def choose(step, what, lo, hi):
        if hi - lo == 1:
            what(lo)
        else:
            mid = (lo + hi) // 2
            lax.cond(
                step < mid, lambda: choose(step, what, lo, mid), lambda: choose(step, what, mid, hi)
            )

    def mm1(step):
        kind, group = unit(MM1, step)
        blocks = pair(kind)
        term = None
        for j in range(2):
            i = 2 * group + j
            left = jnp.concatenate([panel[i, cb] for cb in blocks], axis=0)
            d = lax.dot_general(left, wbuf[i], NT, preferred_element_type=F32)
            term = d if term is None else term + d
        for n, cb in enumerate(blocks):
            acc[cb] = acc[cb] + term[n * ob:(n + 1) * ob]

    def mm1h(step):
        p, group = unit(MM1H, step)
        plane = lax.rem(z + 2, NZ)
        term = None
        for j in range(2):
            i = 2 * group + j
            rows = [
                panel[i, 2 * plane + q // 2, pl.ds(pl.multiple_of(q % 2 * tb + p * hb, hb), hb), :] for q in range(4)
            ]
            d = lax.dot_general(jnp.concatenate(rows, axis=0), wbuf[i], NT, preferred_element_type=F32)
            term = d if term is None else term + d
        acc2[p] = acc2[p] + term

    def mm2(step):
        kind, group = unit(MM2, step)
        blocks = pair(kind)
        left = jnp.concatenate([xt[cb] for cb in blocks], axis=1)
        for j in range(2):
            i = 2 * group + j
            right = jnp.concatenate([panel[i, cb] for cb in blocks], axis=0)
            d = lax.dot_general(left, right, NN, preferred_element_type=F32)
            dw_ref[i] = dw_ref[i] + d

    def sib(kind, group):
        took(blocks_of(2, 2, tb), core_sem.at[kind, group])

    def sib2(p, group):
        took(blocks_of(2, 2, hb), core2_sem.at[p, group])

    def quarter(kind, xc):
        near = xc // 2 == lax.rem(z + (kind in (NEAR, CROSS)), 2)
        h = jnp.where(near, lax.rem(xc, 2), 1 - lax.rem(xc, 2))
        row = pl.multiple_of(jnp.where(near, 0, tb), tb)
        if kind in (OWN, FAR):
            return 2 * lax.rem(z + kind // FAR * 2, NZ) + h, row
        dy = kind - NEAR
        return jnp.where(h == lax.rem(yh + dy, 2), owned(3, dy), owned(1, dy)), row

    def rs_copy(kind, dx):
        cb, row = quarter(kind, lax.rem(x + dx, NX))
        return remote(
            sbuf.at[cb, pl.ds(row, tb), :], rx.at[kind, dx - 1], rs_send, rs_recv.at[kind],
            (r, at_col(0, dx)),
        )

    def rs_start(kind):
        blocks = (2 * z, 2 * z + 1) if kind == OWN else (owned(3, kind - NEAR), owned(1, kind - NEAR))
        for cb in blocks:
            sbuf[cb] = acc[cb].astype(BF16)
        for dx in (1, 2, 3):
            rs_copy(kind, dx).start()

    def to_owner(src, rows, s_sem, cb, j):
        owner_yl, owner_x = cb // NX, lax.rem(cb, NX)
        rel = lax.rem(owner_yl + yl, 2)
        cp = remote(src, parts.at[j, rel, rows[0], rows[1]], s_sem, own_recv.at[j, rel], (r, owner_yl * NX + owner_x))
        return cp, jnp.logical_or(owner_x != x, owner_yl != yl)

    def own_copy(kind):
        cb, row = quarter(kind, x)
        return to_owner(stage.at[kind], (pl.ds(0, tb), slice(None)), own_send.at[kind], cb, row // tb)

    def rs_collect(kind):
        cb, row = quarter(kind, x)
        total = acc[cb, pl.ds(row, tb), :]
        took(rx.at[kind], rs_recv.at[kind])
        for dx in (1, 2, 3):
            total = total + rx[kind, dx - 1].astype(F32)
        stage[kind] = total.astype(BF16)
        cp, away = own_copy(kind)
        pl.when(away)(cp.start)

    dt = acc.shape[2]
    pieces = ((0, 0, dt), (1, 0, dt // 2), (1, dt // 2, dt))

    def rs2_copy(m, dx):
        p, lo, hi = pieces[m]
        cb, row = quarter(FAR, lax.rem(x + dx, NX))
        cols = pl.ds(lo, hi - lo)
        return remote(
            sbuf.at[cb, pl.ds(pl.multiple_of(row + p * hb, hb), hb), cols],
            rx.at[FAR, dx - 1, pl.ds(p * hb, hb), cols],
            rs_send, rs2_recv.at[m], (r, at_col(0, dx)),
        )

    def rs2_start(p):
        plane = lax.rem(z + 2, NZ)
        for q in range(4):
            row = q % 2 * tb + p * hb
            sbuf[2 * plane + q // 2, row:row + hb, :] = acc2[p, q * hb:(q + 1) * hb, :].astype(BF16)
        for m in range(3):
            if pieces[m][0] == p:
                for dx in (1, 2, 3):
                    rs2_copy(m, dx).start()

    def own2_copy(m):
        p, lo, hi = pieces[m]
        cb, row = quarter(FAR, x)
        part, cols = pl.ds(p * hb, hb), pl.ds(lo, hi - lo)
        return to_owner(stage.at[FAR, part, cols], (part, cols), own_send.at[FAR + m], cb, row // tb)

    def rs2_collect(m):
        p, lo, hi = pieces[m]
        cb, row = quarter(FAR, x)
        row = lax.rem(cb, 2) * tb + row // 2
        total = acc2[p, pl.ds(pl.multiple_of(row, hb), hb), lo:hi]
        took(rx.at[FAR, :, pl.ds(p * hb, hb), pl.ds(lo, hi - lo)], rs2_recv.at[m])
        for dx in (1, 2, 3):
            total = total + rx[FAR, dx - 1, p * hb:(p + 1) * hb, lo:hi].astype(F32)
        stage[FAR, p * hb:(p + 1) * hb, lo:hi] = total.astype(BF16)
        cp, away = own2_copy(m)
        pl.when(away)(cp.start)

    def rs_finish():
        offset = lax.rem(c // 2 - z + NZ, NZ)
        beside = NEAR + lax.rem(lax.rem(c, 2) + yh, 2)
        mine = jnp.where(offset == 0, OWN, jnp.where(offset == 2, FAR, beside))

        def arrived(j, rel):
            here = parts.at[j, rel]
            remote(here, here, own_send.at[0], own_recv.at[j, rel], core_other).wait_recv()

        def keep():
            parts[0, 0] = stage[mine]

        pl.when(offset == 1)(lambda: arrived(0, 0))
        pl.when(offset != 1)(keep)
        for j in range(2):
            for rel in range(2):
                if j or rel:
                    arrived(j, rel)
            total = parts[j, 0].astype(F32) + parts[j, 1].astype(F32)
            gi_ref[j * tb:(j + 1) * tb, :] = total.astype(gi_ref.dtype)

    def near(i):
        took(blocks_of(1, 2, tb), recv_sem.at[0, i])
        for dz in (3, 1):
            if i >= NA:
                push(dz, 0, i, y_other, recv_sem.at[1, i])
            share(dz, 0, i)

    def other(i):
        took(blocks_of(1, 1, tb), recv_sem.at[2, i])
        if i < NA:
            push(0, 1, i, z_up, recv_sem.at[1, i])
            push(0, 1, i, z_dn, recv_sem.at[1, i])
        share(0, 1, i)

    def near_other(i):
        took(blocks_of(1, 2, tb), recv_sem.at[1, i])
        for dz in (3, 1):
            share(dz, 1, i)
        if i < NA:
            relay(1, i, 0)

    def far(chunks, halves):
        took(blocks_of(1, len(chunks) * len(halves), hb), far_slot(0, chunks[0], halves[0]))
        for p in halves:
            for i in chunks:
                if i >= NA:
                    push2(2, 0, i, p, y_other, far_slot(1, i, p))
                share2(0, i, p)

    def far_other(group, p):
        took(blocks_of(1, 2, hb), far_slot(1, 2 * group, p))
        for i in GROUPS[group]:
            share2(1, i, p)

    def forward_x():
        took(xbuf.at[pl.ds(0, 1)], x_recv.at[0])
        for dx in (1, 2, 3):
            send_x(at_col(1, 0), (r, at_col(0, dx)), x_recv.at[1])

    def clear(chunks):
        for i in chunks:
            dw_ref[i] = jnp.zeros_like(dw_ref[i])

    def before(n):
        if n == 0:
            acc[...] = jnp.zeros_like(acc)
            acc2[...] = jnp.zeros_like(acc2)
            near(0)
            forward_x()
            clear((0, 1))
            near(1)
            pltpu.make_async_copy(wbuf, wbuf, w_sem).wait()
        if n == 1:
            other(0)
            near(2)
            other(1)
            clear((2, 3))
        if n == 2:
            near(3)
            other(2)
        if n == 3:
            near(4)
            other(3)
            clear((4, 5))
        if n == 6:
            near_other(1)
        if n == 7:
            other(4)
            other(5)
        if n == 8:
            near_other(2)
        if n == 9:
            near_other(3)
            for dy in range(2):
                for i in range(NA):
                    relay(dy, i, 1)
            near_other(4)
        if n == 12:
            far_other(1, 0)
        if n == 13:
            far_other(2, 0)
        if n == 15:
            far_other(0, 1)
        if n == 16:
            far_other(1, 1)
        if MM1[n] is not None:
            sib(*MM1[n])
        if MM1H[n] is not None:
            sib2(*MM1H[n])
        if n == 12:
            rs_collect(NEAR)
        if n == 12:
            rs_collect(OWN)
        if n == 15:
            rs_collect(CROSS)
        if n == 19:
            rs2_collect(0)
        if n == 20:
            rs2_collect(1)
            rs2_collect(2)

    def between(n):
        if n == 3:
            near(5)
            for i in (4, 5):
                for p in range(2):
                    relay(0, i, p)
            for i in range(NA):
                relay(0, i, 0)
            took(xbuf.at[pl.ds(0, 6)], x_recv.at[1])
            for cb in range(2 * NZ):
                xt[cb] = xbuf[cb].T
        if n == 4:
            rs_start(NEAR)
            near_other(0)
        if n == 8:
            rs_start(OWN)
        if n == 10:
            near_other(5)
            far((4, 5), (0, 1))
        if n == 11:
            rs_start(CROSS)
            far((0, 1, 2, 3), (0,))
            far_other(0, 0)
        if n == 13:
            far((0, 1, 2, 3), (1,))
            far_other(2, 1)
        if n == 14:
            rs2_start(0)
        if n == 17:
            rs2_start(1)

    @pl.loop(0, STEPS)
    def _(step):
        choose(step, before, 0, STEPS)
        pl.when(busy(MM1, step))(lambda: mm1(step))
        pl.when(busy(MM1H, step))(lambda: mm1h(step))
        choose(step, between, 0, STEPS)
        pl.when(busy(MM2, step))(lambda: mm2(step))

    rs_finish()

    assert n_sent[0] == N_SENDS and n_sent2[0] == N_SENDS2
    rest = 2 * (N_SENDS - FIRST_SENDS) + N_SENDS2
    for sem, ref in (
        (send_sem.at[0], blocks_of(NCH, FIRST_SENDS // NCH, tb)),
        (send_sem.at[1], blocks_of(NCH, rest // 2 // NCH, tb)),
        (x_send, xbuf.at[pl.ds(0, 7)]),
        (rs_send, rx),
    ):
        remote(ref, ref, sem, recv_sem.at[0, 0], core_other).wait_send()
    last = [own_copy(kind) for kind in (OWN, NEAR, CROSS)] + [own2_copy(m) for m in range(3)]
    for cp, away in last:
        pl.when(away)(cp.wait_send)


N_SENDS = (12 + 8) + (6 + 4) + 36
N_SENDS2 = 20 + 4 + 24
FIRST_SENDS = 48


def out_kernel(gi_ref, dw_ref, gi_out, dw_out, buf, sem):
    rows, cw = dw_ref.shape[1] // 2, dw_ref.shape[2]
    gi_copy = pltpu.make_async_copy(gi_ref, gi_out, sem.at[0])
    gi_copy.start()
    for i in range(NCH):
        for h in range(2):
            part = pl.ds(h * rows, rows)
            buf[i, h * rows:(h + 1) * rows] = dw_ref[i, h * rows:(h + 1) * rows].astype(buf.dtype)
            pltpu.make_async_copy(buf.at[i, part], dw_out.at[part, pl.ds(i * cw, cw)], sem.at[1]).start()
    pltpu.make_async_copy(buf, buf, sem.at[1]).wait()
    gi_copy.wait()


def body(grad_hidden, pre_act, inputs, weight):
    tb, ft = grad_hidden.shape
    ob, dt = inputs.shape
    cw = ft // NCH
    hbm = pl.BlockSpec(memory_space=pltpu.HBM)
    vmem = pl.BlockSpec(memory_space=pltpu.VMEM)
    dma = pltpu.SemaphoreType.DMA
    gi, dw = pl.pallas_call(
        main_kernel,
        out_shape=(pltpu.VMEM((ob, dt), BF16), pltpu.VMEM((NCH, dt, cw), F32)),
        in_specs=[hbm] * 4,
        out_specs=(vmem, vmem),
        scratch_shapes=[
            pltpu.VMEM((NCH, 2, tb, cw), BF16),
            pltpu.VMEM((NCH, 8, ob, cw), BF16),
            pltpu.VMEM((NCH, dt, cw), BF16),
            pltpu.VMEM((8, ob, dt), BF16),
            pltpu.VMEM((8, dt, ob), BF16),
            pltpu.VMEM((8, ob, dt), F32),
            pltpu.VMEM((2, ob, dt), F32),
            pltpu.VMEM((8, ob, dt), BF16),
            pltpu.VMEM((4, NX - 1, tb, dt), BF16),
            pltpu.VMEM((4, tb, dt), BF16),
            pltpu.VMEM((2, 2, tb, dt), BF16),
            dma((2,)),
            dma,
            dma,
            dma((2,)),
            dma((3, NCH)),
            dma((9,)),
            dma((3, 3)),
            dma((2, 3)),
            dma,
            dma((2,)),
            dma,
            dma((3,)),
            dma((3,)),
            dma((6,)),
            dma((2, 2)),
        ],
        compiler_params=pltpu.CompilerParams(
            collective_id=0, has_side_effects=True, vmem_limit_bytes=44 * 2**20
        ),
        name="gather_and_multiply",
    )(grad_hidden, pre_act, inputs, weight)
    return pl.pallas_call(
        out_kernel,
        out_shape=(
            jax.ShapeDtypeStruct((ob, dt), BF16),
            jax.ShapeDtypeStruct((dt, ft), BF16),
        ),
        in_specs=[vmem, vmem],
        out_specs=(hbm, hbm),
        scratch_shapes=[pltpu.VMEM((NCH, dt, cw), BF16), dma((2,))],
        compiler_params=pltpu.CompilerParams(vmem_limit_bytes=20 * 2**20),
        name="round_and_write",
    )(gi, dw)


def solution(mesh):
    return jax.shard_map(
        body,
        mesh=mesh,
        in_specs=(P("row", "col"), P("row", "col"), P("col", "row"), P("row", "col")),
        out_specs=(P("col", "row"), P("row", "col")),
        check_vma=False,
    )
```

```python
import math

import jax
import jax.numpy as jnp
from jax import lax
from jax.experimental import pallas as pl
from jax.experimental.pallas import tpu as pltpu
from jax.sharding import PartitionSpec as P

NZ = 4
NX = 4
NCH = 6
NA = 4
GROUPS = ((0, 1), (2, 3), (4, 5))
OWN, NEAR, CROSS, FAR = range(4)
STEP = (
    ((NEAR, 0), None, None),
    ((OWN, 0), None, None),
    ((NEAR, 1), None, None),
    ((OWN, 1), None, (OWN, 0)),
    ((NEAR, 2), None, (NEAR, 0)),
    (None, None, (OWN, 1)),
    (None, None, (NEAR, 1)),
    ((CROSS, 0), None, (NEAR, 2)),
    ((OWN, 2), None, (OWN, 2)),
    (None, None, (CROSS, 0)),
    ((CROSS, 1), None, (CROSS, 1)),
    ((CROSS, 2), None, None),
    (None, (0, 0), None),
    (None, (0, 1), None),
    (None, (0, 2), None),
    (None, (1, 2), None),
    (None, (1, 0), None),
    (None, (1, 1), (CROSS, 2)),
    (None, None, (FAR, 2)),
    (None, None, (FAR, 0)),
    (None, None, (FAR, 1)),
)
MM1, MM1H, MM2 = zip(*STEP)
STEPS = len(STEP)
NT = (((1,), (1,)), ((), ()))
NN = (((1,), (0,)), ((), ()))
BF16 = jnp.bfloat16
F32 = jnp.float32


def gelu_grad(value):
    coeff = math.sqrt(2.0 / math.pi)
    inner = coeff * (value + 0.044715 * value * value * value)
    tanh_value = jnp.tanh(inner)
    return 0.5 * (1.0 + tanh_value) + 0.5 * value * (1.0 - tanh_value * tanh_value) * coeff * (
        1.0 + 3.0 * 0.044715 * value * value
    )


def main_kernel(
    g_hbm, v_hbm, x_hbm, w_hbm,
    gi_ref, dw_ref,
    gvbuf, panel, wbuf, xbuf, xt, acc, acc2, sbuf, rx, stage, parts,
    load_sem, w_sem, x_own_sem, send_sem, recv_sem, far_sem, core_sem, core2_sem, x_send, x_recv, rs_send, rs_recv,
    rs2_recv, own_send, own_recv,
):
    r = lax.axis_index("row")
    c = lax.axis_index("col")
    z, yh, k = r // 4, (r // 2) % 2, r % 2
    yl, x = c // NX, c % NX
    tb = g_hbm.shape[0]
    cw = panel.shape[3]
    ob = x_hbm.shape[0]

    def at_row(dz, dy, dk):
        return lax.rem(z + dz, NZ) * 4 + lax.rem(yh + dy, 2) * 2 + lax.rem(k + dk, 2)

    def at_col(dyl, dx):
        return lax.rem(yl + dyl, 2) * NX + lax.rem(x + dx, NX)

    z_up, z_dn = (at_row(1, 0, 0), c), (at_row(3, 0, 0), c)
    y_other, core_other = (at_row(0, 1, 0), c), (at_row(0, 0, 1), c)

    x_own = pltpu.make_async_copy(x_hbm, xbuf.at[c], x_own_sem)
    x_own.start()
    for i in range(NCH):
        cols = pl.ds(i * cw, cw)
        for n, src in enumerate((g_hbm, v_hbm)):
            pltpu.make_async_copy(src.at[:, cols], gvbuf.at[i, n], load_sem.at[min(i, 1)]).start()
    barrier = pltpu.get_barrier_semaphore()
    partners = [z_up, z_dn, y_other, core_other, (r, at_col(1, 0))]
    partners += [(r, at_col(0, dx)) for dx in (1, 2, 3)]
    for partner in partners:
        pl.semaphore_signal(barrier, inc=1, device_id=partner, device_id_type=pl.DeviceIdType.MESH)

    def grad_pre(i):
        if i < 2:
            part = gvbuf.at[pl.ds(0, 1) if i == 0 else pl.ds(1, NCH - 1)]
            pltpu.make_async_copy(part, part, load_sem.at[i]).wait()
        value = gvbuf[i, 0].astype(F32) * gelu_grad(gvbuf[i, 1].astype(F32))
        panel[i, 2 * z + yh, pl.ds(pl.multiple_of(k * tb, tb), tb), :] = value.astype(BF16)

    grad_pre(0)
    pl.semaphore_wait(barrier, len(partners))

    hb = tb // 2
    n_sent = [0]
    n_sent2 = [0]

    def remote(src, dst, s_sem, r_sem, target):
        return pltpu.make_async_remote_copy(
            src_ref=src, dst_ref=dst, send_sem=s_sem, recv_sem=r_sem,
            device_id=target, device_id_type=pl.DeviceIdType.MESH,
        )

    def owned(dz, dy):
        return 2 * lax.rem(z + dz, NZ) + lax.rem(yh + dy, 2)

    def block(dz, dy, dk, i):
        rows = pl.ds(pl.multiple_of(lax.rem(k + dk, 2) * tb, tb), tb)
        return panel.at[i, owned(dz, dy), rows, :]

    def half(dz, dy, dk, i, p):
        rows = pl.ds(pl.multiple_of(lax.rem(k + dk, 2) * tb + p * hb, hb), hb)
        return panel.at[i, owned(dz, dy), rows, :]

    def push(dz, dy, i, target, sem):
        here = block(dz, dy, 0, i)
        s_sem = send_sem.at[0 if n_sent[0] < FIRST_SENDS else 1]
        remote(here, here, s_sem, sem, target).start()
        n_sent[0] += 1

    def push2(dz, dy, i, p, target, sem):
        here = half(dz, dy, 0, i, p)
        remote(here, here, send_sem.at[1], sem, target).start()
        n_sent2[0] += 1

    def took(ref, sem):
        remote(ref, ref, send_sem.at[0], sem, core_other).wait_recv()

    def blocks_of(n, m, rows):
        return panel.at[pl.ds(0, n), pl.ds(0, m), pl.ds(0, rows), :]

    def share(dz, dy, i):
        kind = OWN if dz == 0 else NEAR + dy
        push(dz, dy, i, core_other, core_sem.at[kind, i // 2])

    def share2(dy, i, p):
        push2(2, dy, i, p, core_other, core2_sem.at[p, i // 2])

    def far_slot(dy, i, p):
        if dy:
            return far_sem.at[3 + 3 * p + i // 2]
        return far_sem.at[2 if i >= NA else p]

    def relay(dy, i, p):
        if i % 2 == 0:
            push2(3, dy, i, p, z_up, far_slot(dy, i, p))
        else:
            push2(1, dy, i, p, z_dn, far_slot(dy, i, p))

    def send_x(cb, target, rs):
        remote(xbuf.at[cb], xbuf.at[cb], x_send, rs, target).start()

    for i in range(NCH):
        if i:
            grad_pre(i)
        push(0, 0, i, z_up, recv_sem.at[0, i])
        push(0, 0, i, z_dn, recv_sem.at[0, i])
        if i == 0:
            x_own.wait()
            send_x(c, (r, at_col(1, 0)), x_recv.at[0])
            for dx in (1, 2, 3):
                send_x(c, (r, at_col(0, dx)), x_recv.at[1])
        push(0, 0, i, y_other, recv_sem.at[2, i])
        share(0, 0, i)

    for i in range(NCH):
        cols = pl.ds(i * cw, cw)
        cp = pltpu.make_async_copy(w_hbm.at[:, cols], wbuf.at[i], w_sem)
        cp.start()

    def packed(values, step):
        def word(part):
            w = sum(v << (2 * n) for n, v in enumerate(part))
            return jnp.int32(w - (1 << 32) if w >> 31 else w)

        w = jnp.where(step < 16, word(values[:16]), word(values[16:]))
        return lax.shift_right_arithmetic(w, 2 * lax.rem(step, 16)) & 3

    def unit(units, step):
        return packed([u[0] if u else 0 for u in units], step), packed([u[1] if u else 0 for u in units], step)

    def pair(kind):
        def of(own, near, cross, far):
            return jnp.where(kind < 2, jnp.where(kind == 0, own, near), jnp.where(kind == 2, cross, far))

        first = of(2 * z, owned(3, 0), owned(3, 1), 2 * lax.rem(z + 2, NZ))
        second = of(2 * z + 1, owned(1, 0), owned(1, 1), 2 * lax.rem(z + 2, NZ) + 1)
        return first, second

    def busy(units, step):
        return packed([0 if u is None else 1 for u in units], step) == 1

    def choose(step, what, lo, hi):
        if hi - lo == 1:
            what(lo)
        else:
            mid = (lo + hi) // 2
            lax.cond(
                step < mid, lambda: choose(step, what, lo, mid), lambda: choose(step, what, mid, hi)
            )

    def mm1(step):
        kind, group = unit(MM1, step)
        blocks = pair(kind)
        term = None
        for j in range(2):
            i = 2 * group + j
            left = jnp.concatenate([panel[i, cb] for cb in blocks], axis=0)
            d = lax.dot_general(left, wbuf[i], NT, preferred_element_type=F32)
            term = d if term is None else term + d
        for n, cb in enumerate(blocks):
            acc[cb] = acc[cb] + term[n * ob:(n + 1) * ob]

    def mm1h(step):
        p, group = unit(MM1H, step)
        plane = lax.rem(z + 2, NZ)
        term = None
        for j in range(2):
            i = 2 * group + j
            rows = [
                panel[i, 2 * plane + q // 2, pl.ds(pl.multiple_of(q % 2 * tb + p * hb, hb), hb), :] for q in range(4)
            ]
            d = lax.dot_general(jnp.concatenate(rows, axis=0), wbuf[i], NT, preferred_element_type=F32)
            term = d if term is None else term + d
        acc2[p] = acc2[p] + term

    def mm2(step):
        kind, group = unit(MM2, step)
        blocks = pair(kind)
        left = jnp.concatenate([xt[cb] for cb in blocks], axis=1)
        for j in range(2):
            i = 2 * group + j
            right = jnp.concatenate([panel[i, cb] for cb in blocks], axis=0)
            d = lax.dot_general(left, right, NN, preferred_element_type=F32)
            dw_ref[i] = dw_ref[i] + d

    def sib(kind, group):
        took(blocks_of(2, 2, tb), core_sem.at[kind, group])

    def sib2(p, group):
        took(blocks_of(2, 2, hb), core2_sem.at[p, group])

    def quarter(kind, xc):
        near = xc // 2 == lax.rem(z + (kind in (NEAR, CROSS)), 2)
        h = jnp.where(near, lax.rem(xc, 2), 1 - lax.rem(xc, 2))
        row = pl.multiple_of(jnp.where(near, 0, tb), tb)
        if kind in (OWN, FAR):
            return 2 * lax.rem(z + kind // FAR * 2, NZ) + h, row
        dy = kind - NEAR
        return jnp.where(h == lax.rem(yh + dy, 2), owned(3, dy), owned(1, dy)), row

    def rs_copy(kind, dx):
        cb, row = quarter(kind, lax.rem(x + dx, NX))
        return remote(
            sbuf.at[cb, pl.ds(row, tb), :], rx.at[kind, dx - 1], rs_send, rs_recv.at[kind],
            (r, at_col(0, dx)),
        )

    def rs_start(kind):
        blocks = (2 * z, 2 * z + 1) if kind == OWN else (owned(3, kind - NEAR), owned(1, kind - NEAR))
        for cb in blocks:
            sbuf[cb] = acc[cb].astype(BF16)
        for dx in (1, 2, 3):
            rs_copy(kind, dx).start()

    def to_owner(src, rows, s_sem, cb, j):
        owner_yl, owner_x = cb // NX, lax.rem(cb, NX)
        rel = lax.rem(owner_yl + yl, 2)
        cp = remote(src, parts.at[j, rel, rows[0], rows[1]], s_sem, own_recv.at[j, rel], (r, owner_yl * NX + owner_x))
        return cp, jnp.logical_or(owner_x != x, owner_yl != yl)

    def own_copy(kind):
        cb, row = quarter(kind, x)
        return to_owner(stage.at[kind], (pl.ds(0, tb), slice(None)), own_send.at[kind], cb, row // tb)

    def rs_collect(kind):
        cb, row = quarter(kind, x)
        total = acc[cb, pl.ds(row, tb), :]
        took(rx.at[kind], rs_recv.at[kind])
        for dx in (1, 2, 3):
            total = total + rx[kind, dx - 1].astype(F32)
        stage[kind] = total.astype(BF16)
        cp, away = own_copy(kind)
        pl.when(away)(cp.start)

    dt = acc.shape[2]
    pieces = ((0, 0, dt), (1, 0, dt // 2), (1, dt // 2, dt))

    def rs2_copy(m, dx):
        p, lo, hi = pieces[m]
        cb, row = quarter(FAR, lax.rem(x + dx, NX))
        cols = pl.ds(lo, hi - lo)
        return remote(
            sbuf.at[cb, pl.ds(pl.multiple_of(row + p * hb, hb), hb), cols],
            rx.at[FAR, dx - 1, pl.ds(p * hb, hb), cols],
            rs_send, rs2_recv.at[m], (r, at_col(0, dx)),
        )

    def rs2_start(p):
        plane = lax.rem(z + 2, NZ)
        for q in range(4):
            row = q % 2 * tb + p * hb
            sbuf[2 * plane + q // 2, row:row + hb, :] = acc2[p, q * hb:(q + 1) * hb, :].astype(BF16)
        for m in range(3):
            if pieces[m][0] == p:
                for dx in (1, 2, 3):
                    rs2_copy(m, dx).start()

    def own2_copy(m):
        p, lo, hi = pieces[m]
        cb, row = quarter(FAR, x)
        part, cols = pl.ds(p * hb, hb), pl.ds(lo, hi - lo)
        return to_owner(stage.at[FAR, part, cols], (part, cols), own_send.at[FAR + m], cb, row // tb)

    def rs2_collect(m):
        p, lo, hi = pieces[m]
        cb, row = quarter(FAR, x)
        row = lax.rem(cb, 2) * tb + row // 2
        total = acc2[p, pl.ds(pl.multiple_of(row, hb), hb), lo:hi]
        took(rx.at[FAR, :, pl.ds(p * hb, hb), pl.ds(lo, hi - lo)], rs2_recv.at[m])
        for dx in (1, 2, 3):
            total = total + rx[FAR, dx - 1, p * hb:(p + 1) * hb, lo:hi].astype(F32)
        stage[FAR, p * hb:(p + 1) * hb, lo:hi] = total.astype(BF16)
        cp, away = own2_copy(m)
        pl.when(away)(cp.start)

    def rs_finish():
        offset = lax.rem(c // 2 - z + NZ, NZ)
        beside = NEAR + lax.rem(lax.rem(c, 2) + yh, 2)
        mine = jnp.where(offset == 0, OWN, jnp.where(offset == 2, FAR, beside))

        def arrived(j, rel):
            here = parts.at[j, rel]
            remote(here, here, own_send.at[0], own_recv.at[j, rel], core_other).wait_recv()

        def keep():
            parts[0, 0] = stage[mine]

        pl.when(offset == 1)(lambda: arrived(0, 0))
        pl.when(offset != 1)(keep)
        for j in range(2):
            for rel in range(2):
                if j or rel:
                    arrived(j, rel)
            total = parts[j, 0].astype(F32) + parts[j, 1].astype(F32)
            gi_ref[j * tb:(j + 1) * tb, :] = total.astype(gi_ref.dtype)

    def near(i):
        took(blocks_of(1, 2, tb), recv_sem.at[0, i])
        for dz in (3, 1):
            if i >= NA:
                push(dz, 0, i, y_other, recv_sem.at[1, i])
            share(dz, 0, i)

    def other(i):
        took(blocks_of(1, 1, tb), recv_sem.at[2, i])
        if i < NA:
            push(0, 1, i, z_up, recv_sem.at[1, i])
            push(0, 1, i, z_dn, recv_sem.at[1, i])
        share(0, 1, i)

    def near_other(i):
        took(blocks_of(1, 2, tb), recv_sem.at[1, i])
        for dz in (3, 1):
            share(dz, 1, i)
        if i < NA:
            relay(1, i, 0)

    def far(chunks, halves):
        took(blocks_of(1, len(chunks) * len(halves), hb), far_slot(0, chunks[0], halves[0]))
        for p in halves:
            for i in chunks:
                if i >= NA:
                    push2(2, 0, i, p, y_other, far_slot(1, i, p))
                share2(0, i, p)

    def far_other(group, p):
        took(blocks_of(1, 2, hb), far_slot(1, 2 * group, p))
        for i in GROUPS[group]:
            share2(1, i, p)

    def forward_x():
        took(xbuf.at[pl.ds(0, 1)], x_recv.at[0])
        for dx in (1, 2, 3):
            send_x(at_col(1, 0), (r, at_col(0, dx)), x_recv.at[1])

    def clear(chunks):
        for i in chunks:
            dw_ref[i] = jnp.zeros_like(dw_ref[i])

    def before(n):
        if n == 0:
            acc[...] = jnp.zeros_like(acc)
            acc2[...] = jnp.zeros_like(acc2)
            near(0)
            forward_x()
            clear((0, 1))
            near(1)
            pltpu.make_async_copy(wbuf, wbuf, w_sem).wait()
        if n == 1:
            other(0)
            near(2)
            other(1)
            clear((2, 3))
        if n == 2:
            near(3)
            other(2)
        if n == 3:
            near(4)
            other(3)
            clear((4, 5))
        if n == 6:
            near_other(1)
        if n == 7:
            other(4)
            other(5)
        if n == 8:
            near_other(2)
        if n == 9:
            near_other(3)
            for dy in range(2):
                for i in range(NA):
                    relay(dy, i, 1)
            near_other(4)
        if n == 12:
            far_other(1, 0)
        if n == 13:
            far_other(2, 0)
        if n == 15:
            far_other(0, 1)
        if n == 16:
            far_other(1, 1)
        if MM1[n] is not None:
            sib(*MM1[n])
        if MM1H[n] is not None:
            sib2(*MM1H[n])
        if n == 12:
            rs_collect(NEAR)
        if n == 12:
            rs_collect(OWN)
        if n == 15:
            rs_collect(CROSS)
        if n == 18:
            rs2_collect(0)
        if n == 20:
            rs2_collect(1)
            rs2_collect(2)

    def between(n):
        if n == 3:
            near(5)
            for i in (4, 5):
                for p in range(2):
                    relay(0, i, p)
            for i in range(NA):
                relay(0, i, 0)
            took(xbuf.at[pl.ds(0, 6)], x_recv.at[1])
            for cb in range(2 * NZ):
                xt[cb] = xbuf[cb].T
        if n == 4:
            rs_start(NEAR)
            near_other(0)
        if n == 8:
            rs_start(OWN)
        if n == 10:
            near_other(5)
            far((4, 5), (0, 1))
        if n == 11:
            rs_start(CROSS)
            far((0, 1, 2, 3), (0,))
            far_other(0, 0)
        if n == 13:
            far((0, 1, 2, 3), (1,))
            far_other(2, 1)
        if n == 14:
            rs2_start(0)
        if n == 17:
            rs2_start(1)

    @pl.loop(0, STEPS)
    def _(step):
        choose(step, before, 0, STEPS)
        pl.when(busy(MM1, step))(lambda: mm1(step))
        pl.when(busy(MM1H, step))(lambda: mm1h(step))
        choose(step, between, 0, STEPS)
        pl.when(busy(MM2, step))(lambda: mm2(step))

    rs_finish()

    assert n_sent[0] == N_SENDS and n_sent2[0] == N_SENDS2
    rest = 2 * (N_SENDS - FIRST_SENDS) + N_SENDS2
    for sem, ref in (
        (send_sem.at[0], blocks_of(NCH, FIRST_SENDS // NCH, tb)),
        (send_sem.at[1], blocks_of(NCH, rest // 2 // NCH, tb)),
        (x_send, xbuf.at[pl.ds(0, 7)]),
        (rs_send, rx),
    ):
        remote(ref, ref, sem, recv_sem.at[0, 0], core_other).wait_send()
    last = [own_copy(kind) for kind in (OWN, NEAR, CROSS)] + [own2_copy(m) for m in range(3)]
    for cp, away in last:
        pl.when(away)(cp.wait_send)


N_SENDS = (12 + 8) + (6 + 4) + 36
N_SENDS2 = 20 + 4 + 24
FIRST_SENDS = 48


def out_kernel(gi_ref, dw_ref, gi_out, dw_out, buf, sem):
    rows, cw = dw_ref.shape[1] // 2, dw_ref.shape[2]
    gi_copy = pltpu.make_async_copy(gi_ref, gi_out, sem.at[0])
    gi_copy.start()
    for i in range(NCH):
        for h in range(2):
            part = pl.ds(h * rows, rows)
            buf[i, h * rows:(h + 1) * rows] = dw_ref[i, h * rows:(h + 1) * rows].astype(buf.dtype)
            pltpu.make_async_copy(buf.at[i, part], dw_out.at[part, pl.ds(i * cw, cw)], sem.at[1]).start()
    pltpu.make_async_copy(buf, buf, sem.at[1]).wait()
    gi_copy.wait()


def body(grad_hidden, pre_act, inputs, weight):
    tb, ft = grad_hidden.shape
    ob, dt = inputs.shape
    cw = ft // NCH
    hbm = pl.BlockSpec(memory_space=pltpu.HBM)
    vmem = pl.BlockSpec(memory_space=pltpu.VMEM)
    dma = pltpu.SemaphoreType.DMA
    gi, dw = pl.pallas_call(
        main_kernel,
        out_shape=(pltpu.VMEM((ob, dt), BF16), pltpu.VMEM((NCH, dt, cw), F32)),
        in_specs=[hbm] * 4,
        out_specs=(vmem, vmem),
        scratch_shapes=[
            pltpu.VMEM((NCH, 2, tb, cw), BF16),
            pltpu.VMEM((NCH, 8, ob, cw), BF16),
            pltpu.VMEM((NCH, dt, cw), BF16),
            pltpu.VMEM((8, ob, dt), BF16),
            pltpu.VMEM((8, dt, ob), BF16),
            pltpu.VMEM((8, ob, dt), F32),
            pltpu.VMEM((2, ob, dt), F32),
            pltpu.VMEM((8, ob, dt), BF16),
            pltpu.VMEM((4, NX - 1, tb, dt), BF16),
            pltpu.VMEM((4, tb, dt), BF16),
            pltpu.VMEM((2, 2, tb, dt), BF16),
            dma((2,)),
            dma,
            dma,
            dma((2,)),
            dma((3, NCH)),
            dma((9,)),
            dma((3, 3)),
            dma((2, 3)),
            dma,
            dma((2,)),
            dma,
            dma((3,)),
            dma((3,)),
            dma((6,)),
            dma((2, 2)),
        ],
        compiler_params=pltpu.CompilerParams(
            collective_id=0, has_side_effects=True, vmem_limit_bytes=44 * 2**20
        ),
        name="gather_and_multiply",
    )(grad_hidden, pre_act, inputs, weight)
    return pl.pallas_call(
        out_kernel,
        out_shape=(
            jax.ShapeDtypeStruct((ob, dt), BF16),
            jax.ShapeDtypeStruct((dt, ft), BF16),
        ),
        in_specs=[vmem, vmem],
        out_specs=(hbm, hbm),
        scratch_shapes=[pltpu.VMEM((NCH, dt, cw), BF16), dma((2,))],
        compiler_params=pltpu.CompilerParams(vmem_limit_bytes=20 * 2**20),
        name="round_and_write",
    )(gi, dw)


def solution(mesh):
    return jax.shard_map(
        body,
        mesh=mesh,
        in_specs=(P("row", "col"), P("row", "col"), P("col", "row"), P("row", "col")),
        out_specs=(P("col", "row"), P("row", "col")),
        check_vma=False,
    )
```
